128 devices in a mesh: dp: 32 (over z, y, core), tensor: 4 (over x).
Axes of the slice: x: 4, y: 4, z: 4, core: 2. Of those that a mesh axis runs over, the one named last changes fastest.
Arguments:
- old_weights: float32 [3, 1024, 16384], P(None, ('dp', 'tensor')), may hold values from -0.046875 to 0.046875
- old_first: float32 [3, 1024, 16384], P(None, ('dp', 'tensor')), may hold values from -6 to 6
- old_second: float32 [3, 1024, 16384], P(None, ('dp', 'tensor')), may hold values from 0.01 to 1
- old_blocks: int32 [128], replicated, may hold values from 0 to 2, as said below
- owner_map: int32 [128, 4], replicated, may hold values from 0 to 3, each once within a row
- inputs: bfloat16 [2, 7680, 16384], P(None, 'dp', 'tensor'), may hold values from -6 to 6
- cotangent: bfloat16 [2, 7680, 16384], P(None, 'dp'), may hold values from -0.19921875 to 0.19921875
Outputs:
- new_weights: float32 [16384, 3, 512], P('dp', None, 'tensor')
- new_first: float32 [16384, 3, 512], P('dp', None, 'tensor')
- new_second: float32 [16384, 3, 512], P('dp', None, 'tensor')
The draws below stay inside these ranges and needn't reach their ends.
Inputs may be any that keep to these rules, and one draw needn't show every extreme that they name: `old_blocks`: pairs of old shards (2 p, 2 p + 1) together hold 2 groups; the counts sum to 128; shard 0 holds 2.
All inputs are finite; a program needn't handle non-finite values.
Results may differ from the reference program's by a relative error of at most 0.03.
Values may be sent and summed in bfloat16 or wider, within the bound.
A program may use at most 128 MiB of HBM per device.

```python
import math
import jax
import jax.numpy as jnp
from jax import lax

D = 16384
TOK_DEV = 240
MICRO = 2
TOKENS = 7680
HOWN = 128
SLOTU = 8
N_DP = 32
N_TENSOR = 4


def draw_old_blocks(key, part):
    key = jax.random.fold_in(key, 11)
    shards = N_DP * N_TENSOR
    pairs = shards // 2
    mean = HOWN // shards
    shift = jax.random.randint(key, (pairs,), -mean, mean + 1)
    shift = shift.at[0].set(mean)
    return jnp.stack([mean + shift, mean - shift], axis=1).reshape(shards).astype(jnp.int32)


def strengthened(entries, key, source, target, parts, factor):
    def block_of(axis_at):
        return (jnp.arange(entries.shape[axis_at]) // (entries.shape[axis_at] // parts)).reshape((-1,) + (1,) * (entries.ndim - 1 - axis_at))

    near = jax.random.permutation(key, parts)[block_of(target)]
    other_side = (block_of(target) + parts // 2) % parts
    return jnp.where((block_of(source) == near) | (block_of(source) == other_side), factor * entries, entries)


def block_scale(rng, dims, split, low, high):
    def one(position, shards_of):
        heights = jax.random.uniform(jax.random.fold_in(jax.random.fold_in(rng, 6), position), (shards_of,), jnp.float32, low / len(split), high / len(split))
        return jnp.repeat(jnp.exp(heights), dims[position] // shards_of).reshape((-1,) + (1,) * (len(dims) - position - 1))

    level = one(*split[0])
    for cut in split[1:]:
        level = level * one(*cut)
    return level


def gaussian(stream_key, dims, deviation, most, pieces=(), kind=jnp.bfloat16):
    array = deviation * jax.random.normal(stream_key, dims, jnp.float32)
    if pieces:
        array = array * block_scale(stream_key, dims, pieces, -0.22, 0.18)
    return jnp.clip(array, -most, most).astype(kind)


def gaussian_with(key, shape, deviation, bound, cuts, heavy, kind=jnp.bfloat16):
    entries = deviation * jax.random.normal(key, shape, jnp.float32)
    if cuts:
        entries = entries * block_scale(key, shape, cuts, -0.22, 0.18)
    return jnp.clip(strengthened(entries, jax.random.fold_in(key, 3), *heavy), -bound, bound).astype(kind)


def setup_inputs(seed: int = 0) -> dict:
    streams_of = jax.random.split(jax.random.key(seed), 8)
    old_weights = gaussian(streams_of[0], (3, N_DP * N_TENSOR * SLOTU, D), D ** -0.5, 0.046875, ((1, 128),), jnp.float32)
    old_first = gaussian(streams_of[1], (3, N_DP * N_TENSOR * SLOTU, D), 1.0, 6.0, ((1, 128),), jnp.float32)
    old_second = jnp.clip(jnp.exp(math.log(1.0) - 4.6051702 * jax.random.uniform(streams_of[2], (3, N_DP * N_TENSOR * SLOTU, D), jnp.float32) ** block_scale(streams_of[2], (3, N_DP * N_TENSOR * SLOTU, D), ((1, 128),), -0.2, 0.2)), 0.01, 1.0)
    old_blocks = draw_old_blocks(jax.random.fold_in(streams_of[7], 71), 0)
    owner_map = jax.vmap(lambda own: jax.random.permutation(own, N_TENSOR))(jax.random.split(streams_of[4], HOWN)).reshape((HOWN, N_TENSOR)).astype(jnp.int32)
    inputs = gaussian_with(streams_of[5], (MICRO, TOKENS, D), 1.0, 6.0, ((1, 32), (2, 4)), (1, 2, 32, 2.75))
    cotangent = gaussian_with(streams_of[6], (MICRO, TOKENS, D), 0.03, 0.19921875, ((1, 32),), (1, 2, 32, 2.75))
    return dict(old_weights=old_weights, old_first=old_first, old_second=old_second, old_blocks=old_blocks, owner_map=owner_map, inputs=inputs, cotangent=cotangent)


def relaid(old, old_blocks, owner_map):
    groups = owner_map.shape[0]
    members = owner_map.shape[1]
    slot_units = old.shape[1] // old_blocks.shape[0]
    ends = jnp.cumsum(old_blocks).astype(jnp.int32)
    starts = (ends - old_blocks).astype(jnp.int32)
    blocks = jnp.arange(groups, dtype=jnp.int32)
    holder = lax.optimization_barrier(jnp.sum((ends[None, :] <= blocks[:, None]).astype(jnp.int32), axis=1)).astype(jnp.int32)
    first = starts[holder]
    owners = jnp.arange(members, dtype=jnp.int32)
    equal = (owner_map[:, None, :] == owners[None, :, None]).astype(jnp.int32)
    place = lax.optimization_barrier(jnp.sum(equal * owners[None, None, :], axis=2)).astype(jnp.int32)
    base = holder * slot_units + members * (blocks - first)
    index = (base[None, :] + place.T).reshape(-1).astype(jnp.int32)
    chosen = jnp.take(old, index, axis=1)
    return jnp.transpose(chosen, (2, 0, 1))

def silu_parts(gate):
    sig = jax.nn.sigmoid(gate)
    return (gate * sig, sig * (1.0 + gate * (1.0 - sig)))

def contract_rows(left, right):
    return lax.dot_general(left, right, (((0,), (0,)), ((), ())), preferred_element_type=jnp.float32)

def reference(old_weights, old_first, old_second, old_blocks, owner_map, inputs, cotangent):
    weights = relaid(old_weights, old_blocks, owner_map)
    first = relaid(old_first, old_blocks, owner_map)
    second = relaid(old_second, old_blocks, owner_map)
    half = weights.astype(jnp.bfloat16)
    width = half.shape[0]
    units = half.shape[2]

    def one_group(total, index):
        start = (index * TOK_DEV).astype(jnp.int32)
        tokens = lax.dynamic_slice_in_dim(inputs, start, TOK_DEV, 1).reshape(MICRO * TOK_DEV, width)
        backs = lax.dynamic_slice_in_dim(cotangent, start, TOK_DEV, 1).reshape(MICRO * TOK_DEV, width)
        gate = jnp.dot(tokens, half[:, 0, :], preferred_element_type=jnp.float32)
        up = jnp.dot(tokens, half[:, 1, :], preferred_element_type=jnp.float32)
        back = jnp.dot(backs, half[:, 2, :], preferred_element_type=jnp.float32)
        act, slope = silu_parts(gate)
        hidden = (act * up).astype(jnp.bfloat16)
        dgate = (back * up * slope).astype(jnp.bfloat16)
        dup = (back * act).astype(jnp.bfloat16)
        term = jnp.stack([contract_rows(tokens, dgate), contract_rows(tokens, dup), contract_rows(backs, hidden)], axis=1)
        rounded = lax.optimization_barrier(term.astype(jnp.bfloat16))
        return (total + rounded.astype(jnp.float32), None)
    start_total = jnp.zeros((width, 3, units), jnp.float32)
    grad, _ = lax.scan(one_group, start_total, jnp.arange(N_DP, dtype=jnp.int32))
    new_first = 0.9 * first + 0.1 * grad
    new_second = 0.95 * second + 0.05 * grad * grad
    new_weights = weights - 8e-05 * (new_first / (jnp.sqrt(new_second) + 1e-08) + 0.1 * weights)
    return (new_weights, new_first, new_second)
```

```python
import functools

import jax
import jax.numpy as jnp
from jax import lax
from jax.experimental import pallas as pl
from jax.experimental.pallas import tpu as pltpu
from jax.sharding import Mesh, PartitionSpec as P

BF = jnp.bfloat16
F32 = jnp.float32
MESH = pl.DeviceIdType.MESH
NS = 256


def dot_nt(a, b):
    return lax.dot_general(a, b, (((1,), (1,)), ((), ())), preferred_element_type=F32)


def dot(a, b):
    return jnp.dot(a, b, preferred_element_type=F32)


def iota(shape, dim):
    return lax.broadcasted_iota(jnp.int32, shape, dim)


def kernel(
    blocks, owners, old_w, old_f, old_s, tok_in, cot_in,
    out_w, out_f, out_s,
    stage, xs, xr, mom, yx, swp, fin, wall, tok, cot, part, part_in, sgr, grd, r1, r2, ysum, r3, r4, zed,
    sel_a, sel_b, perm, perm64, perm128,
    ssem, rsem, lsem,
):
    z, y, c, x = (lax.axis_index(a) for a in ("z", "y", "c", "x"))
    step4 = lambda v, d: lax.rem(v + d + 4, 4)
    counter = [0]
    started = []

    def copy(src, dst, dev):
        n = counter[0]
        counter[0] += 1
        d = pltpu.make_async_remote_copy(
            src_ref=src, dst_ref=dst, send_sem=ssem.at[n], recv_sem=rsem.at[n],
            device_id=dev, device_id_type=MESH,
        )
        d.start()
        started.append(d)
        return d

    barrier = pltpu.get_barrier_semaphore()

    def greet(dev):
        pl.semaphore_signal(barrier, inc=1, device_id=dev, device_id_type=MESH)

    for d in (1, 2, 3):
        greet({"x": step4(x, d)})
        greet({"y": step4(y, d)})
    for d in (1, 3):
        greet({"z": step4(z, d)})
    greet({"c": 1 - c})
    for zs in range(4):
        for cs in range(2):
            greet({"x": z, "z": zs, "c": cs})

    olds = (old_w, old_f, old_s)
    local = []

    def load(src, dst):
        d = pltpu.make_async_copy(src, dst, lsem.at[len(local)])
        d.start()
        local.append(d)
        return d

    loads = [load(olds[k // 3].at[k % 3], stage.at[k]) for k in range(9)]
    quarter = pl.ds(pl.multiple_of(x * 4096, 4096), 4096)
    tload = []
    for mb in range(2):
        rows = pl.ds(240 * mb, 240)
        tload.append(load(tok_in.at[rows], tok.at[2 * c + mb, pl.ds(0, 240)]))
        tload.append(load(cot_in.at[rows, quarter], cot.at[2 * c + mb, pl.ds(0, 240)]))
    tok[:, 240:, :] = jnp.zeros((4, 16, 4096), BF)
    cot[:, 240:, :] = jnp.zeros((4, 16, 4096), BF)

    shape = (16, 64)
    row, col = iota(shape, 0), iota(shape, 1)
    ru, ri = row // 4, row % 4
    cx, ch, cj, cs = col // 16, (col // 8) % 2, (col // 4) % 2, col % 4
    dp = z * 8 + y * 2 + c
    group = jnp.full(shape, -1, jnp.int32)
    for xx in range(4):
        held = blocks[dp * 4 + xx]
        base = 2 * (xx // 2) + (blocks[dp * 4 + xx - 1] if xx % 2 else 0)
        for j in range(2):
            group = jnp.where((cx == xx) & (cj == j), jnp.where(j < held, base + j, -1), group)
    who = jnp.full(shape, -1, jnp.int32)
    for i in range(4):
        for s in range(4):
            who = jnp.where((ri == i) & (cs == s), owners[s, dp * 4 + i], who)
    hit = (group == ri) & (who == ru)
    sel_a[...] = jnp.where(hit & (ch == 0), 1.0, 0.0).astype(BF)
    sel_b[...] = jnp.where(hit & (ch == 1), 1.0, 0.0).astype(BF)
    r, q = iota((64, 64), 0), iota((64, 64), 1)
    want = ((r // 4) % 4) * 16 + (r // 16) * 4 + r % 4
    perm64[...] = jnp.where(q == want, 1.0, 0.0).astype(BF)
    r, q = iota((256, 256), 0), iota((256, 256), 1)
    want = (r // 64) * 64 + ((r // 4) % 4) * 16 + ((r // 16) % 4) * 4 + r % 4
    perm[...] = jnp.where(q == want, 1.0, 0.0).astype(BF)
    r, q = iota((128, 128), 0), iota((128, 128), 1)
    want = (r // 32) * 32 + ((r // 4) % 2) * 16 + ((r // 8) % 4) * 4 + r % 4
    perm128[...] = jnp.where(q == want, 1.0, 0.0).astype(BF)

    def pack(k):
        loads[k].wait()
        for xx in range(4):
            lo = stage[k, :, xx * 4096 : xx * 4096 + 2048]
            hi = stage[k, :, xx * 4096 + 2048 : xx * 4096 + 4096]
            xs[k, xx] = jnp.concatenate([lo, hi], axis=0).astype(BF)
        xr[k, x] = xs[k, x]

    pack(0)
    pl.semaphore_wait(barrier, 17)

    xcop = {}

    def xsend(k, n):
        ks = pl.ds(k, n)
        for d in (1, 3, 2):
            xcop[k, d] = copy(xs.at[ks, step4(x, d)], xr.at[ks, x], {"x": step4(x, d)})

    xsend(0, 1)
    sib = {"c": 1 - c}
    mine = []
    for mb in range(2):
        rows = pl.ds(240 * mb, 240)
        mine.append(copy(tok_in.at[rows], tok.at[2 * c + mb, pl.ds(0, 240)], sib))
    pack(1)
    xsend(1, 1)
    pack(2)
    xsend(2, 1)
    mine_cot = []
    for mb in range(2):
        rows = pl.ds(240 * mb, 240)
        mine_cot.append(copy(cot_in.at[rows, quarter], cot.at[2 * c + mb, pl.ds(0, 240)], sib))

    def xwait(k):
        for d in (1, 3, 2):
            xcop[k, d].wait_recv()

    def select(k):
        rows = xr[k].reshape(64, 2048)
        return dot(sel_a[...], rows).astype(BF), dot(sel_b[...], rows).astype(BF)

    def wref(m, h, first, second, lo, n):
        cols = pl.ds(2048 * h + lo, n)
        if h == 0:
            return wall.at[m, second, first, :, cols]
        return wall.at[m, first, second, :, cols]

    def ring1(h, d):
        return {"y": step4(y, d)} if h == 0 else {"z": step4(z, d)}

    def ring2(h, d):
        return {"z": step4(z, d)} if h == 0 else {"y": step4(y, d)}

    def at1(h, d):
        return step4(y if h == 0 else z, d)

    def at2(h, d):
        return step4(z if h == 0 else y, d)

    ag = {}
    ITEM = (0, -1, 1, 2)

    def out2(m, h, j):
        piece = wref(m, h, at1(h, ITEM[j]), at2(h, 0), 0, 2048)
        ag[m, h, j, "l"] = copy(piece, piece, ring2(h, 1))
        ag[m, h, j, "r"] = copy(piece, piece, ring2(h, -1))

    def ag1(m):
        xwait(m)
        a, b = select(m)
        wall[m, z, y, :, 0:2048] = a
        wall[m, z, y, :, 2048:4096] = b
        for yy in range(4):
            half = a if yy < 2 else b
            mom[m, yy] = half[:, 1024 * (yy % 2) : 1024 * (yy % 2) + 1024]
        for h in range(2):
            piece = wref(m, h, at1(h, 0), at2(h, 0), 0, 2048)
            ag[m, h, "l"] = copy(piece, piece, ring1(h, 1))
            ag[m, h, "r"] = copy(piece, piece, ring1(h, -1))
        for h in range(2):
            out2(m, h, 0)

    def ag2(m):
        for h in range(2):
            ag[m, h, "l"].wait_recv()
            piece = wref(m, h, at1(h, -1), at2(h, 0), 0, 1024)
            ag[m, h, "fl"] = copy(piece, piece, ring1(h, 1))
            ag[m, h, "r"].wait_recv()
            piece = wref(m, h, at1(h, 1), at2(h, 0), 1024, 1024)
            ag[m, h, "fr"] = copy(piece, piece, ring1(h, -1))
        for h in range(2):
            out2(m, h, 1)
            out2(m, h, 2)

    def forward(m, h, j):
        ag[m, h, j, "l"].wait_recv()
        piece = wref(m, h, at1(h, ITEM[j]), at2(h, -1), 0, 1024)
        ag[m, h, j, "fl"] = copy(piece, piece, ring2(h, 1))
        ag[m, h, j, "r"].wait_recv()
        piece = wref(m, h, at1(h, ITEM[j]), at2(h, 1), 1024, 1024)
        ag[m, h, j, "fr"] = copy(piece, piece, ring2(h, -1))

    def ag3(m):
        for h in range(2):
            ag[m, h, "fl"].wait_recv()
            ag[m, h, "fr"].wait_recv()
            out2(m, h, 3)
        for h in range(2):
            forward(m, h, 0)

    def ag4(m):
        for h in range(2):
            forward(m, h, 1)
            forward(m, h, 2)

    def ag5(m):
        for h in range(2):
            forward(m, h, 3)

    def ag6(m):
        for h in range(2):
            for j in range(4):
                ag[m, h, j, "fl"].wait_recv()
                ag[m, h, j, "fr"].wait_recv()

    pc = {}

    def fwd(m):
        acts = cot if m == 2 else tok

        def body(b, carry):
            part[m, b] = dot_nt(acts[b], wall[m].reshape(256, 4096)).astype(BF)
            return carry

        lax.fori_loop(0, 4, body, 0)
        for d in (1, 3, 2):
            pc[m, d] = copy(part.at[m, step4(x, d)], part_in.at[m, d - 1], {"x": step4(x, d)})

    def summed(m):
        for d in (1, 3, 2):
            pc[m, d].wait_recv()
        total = part[m, x].astype(F32)
        for d in range(3):
            total = total + part_in[m, d].astype(F32)
        return total

    sc = {}

    def share(m, value):
        sgr[m, x] = dot_nt(perm[...], value.astype(BF)).astype(BF)
        for d in (1, 3, 2):
            sc[m, d] = copy(sgr.at[m, x], sgr.at[m, x], {"x": step4(x, d)})

    def bwd(m):
        acts = cot if m == 2 else tok
        for d in (1, 3, 2):
            sc[m, d].wait_recv()

        def body(n, carry):
            cols = pl.ds(pl.multiple_of(n * 512, 512), 512)
            left = jnp.concatenate([sgr[m, b] for b in range(4)], axis=1)
            right = acts[:, :, cols].reshape(1024, 512)
            res = dot(left, right).astype(BF).reshape(4, 64, 512)
            grd[m, lax.rem(n, 2), n // 2] = res
            return carry

        lax.fori_loop(0, 8, body, 0)

    rs = {}

    def gref(m, h, p, q):
        return (m, h, q, p) if h == 0 else (m, h, p, q)

    def rs1(m):
        for h in range(2):
            far = at2(h, 2)
            for half in range(2):
                if h == 0:
                    src = grd.at[m, h, pl.ds(2 * half, 2), far]
                else:
                    src = grd.at[m, h, far, pl.ds(2 * half, 2)]
                rs[m, h, 1, half] = copy(src, r1.at[m, h, half], ring2(h, 1 if half == 0 else -1))

    def rs2(m):
        for h in range(2):
            for half in range(2):
                rs[m, h, 1, half].wait_recv()
                to = 1 if half == 0 else -1
                p = at2(h, to)
                for k in range(2):
                    at = gref(m, h, p, 2 * half + k)
                    grd[at] = (grd[at].astype(F32) + r1[m, h, half, k].astype(F32)).astype(BF)
                src = grd.at[m, h, :, p] if h == 0 else grd.at[m, h, p]
                rs[m, h, 2, half] = copy(src, r2.at[m, h, half], ring2(h, to))

    def rs3(m):
        for h in range(2):
            rs[m, h, 2, 0].wait_recv()
            rs[m, h, 2, 1].wait_recv()
            for q in range(4):
                own = grd[gref(m, h, at2(h, 0), q)].astype(F32)
                ysum[m, h, q] = (
                    own + r2[m, h, 0, q].astype(F32) + r2[m, h, 1, q].astype(F32)
                ).astype(BF)
            for half in range(2):
                src = ysum.at[m, h, at1(h, 2), pl.ds(32 * half, 32)]
                rs[m, h, 3, half] = copy(src, r3.at[m, h, half], ring1(h, 1 if half == 0 else -1))

    def rs4(m):
        for h in range(2):
            for half in range(2):
                rs[m, h, 3, half].wait_recv()
                to = 1 if half == 0 else -1
                p = at1(h, to)
                rows = pl.ds(32 * half, 32)
                ysum[m, h, p, rows] = (
                    ysum[m, h, p, rows].astype(F32) + r3[m, h, half].astype(F32)
                ).astype(BF)
                rs[m, h, 4, half] = copy(ysum.at[m, h, p], r4.at[m, h, half], ring1(h, to))

    def deliver(base, ref_of, dst):
        n0 = counter[0]
        counter[0] += 8
        pending = []
        for u in range(4):
            for h in range(2):
                same = (x == z) & (x == u) & (c == h)
                remote = pltpu.make_async_remote_copy(
                    src_ref=ref_of(u, h), dst_ref=dst, send_sem=ssem.at[n0 + u * 2 + h],
                    recv_sem=rsem.at[n0], device_id={"x": u, "z": x, "c": h}, device_id_type=MESH,
                )
                pending.append((same, remote))

                @pl.when(jnp.logical_not(same))
                def _():
                    remote.start()

                @pl.when(same)
                def _():
                    pltpu.make_async_copy(ref_of(u, h), dst, rsem.at[n0]).start()

        return n0, pending

    late = []
    gsem = {}

    def rs5(m):
        for h in range(2):
            rs[m, h, 4, 0].wait_recv()
            rs[m, h, 4, 1].wait_recv()
            own = ysum[m, h, at1(h, 0)].astype(F32)
            zed[m, h] = (
                own + r4[m, h, 0].astype(F32) + r4[m, h, 1].astype(F32)
            ).astype(BF).reshape(4, 16, 512)
        n0, pending = deliver(
            9 + m, lambda u, h: zed.at[m, h, u], fin.at[9 + m, z * 2 + c]
        )
        gsem[m] = n0
        late.extend(pending)

    def landed(n0, k, n):
        whole = fin.at[pl.ds(k, n)]
        pltpu.make_async_copy(whole, whole, rsem.at[n0]).wait()

    yc = {}
    msem = {}

    def mom_pick(a):
        xwait(3 * a)
        for k in range(3 * a, 3 * a + 3):
            lo, hi = select(k)
            for yy in range(4):
                half = lo if yy < 2 else hi
                mom[k, yy] = half[:, 1024 * (yy % 2) : 1024 * (yy % 2) + 1024]

    def mom_y():
        yx[y] = mom[:, y]
        for d in (1, 3, 2):
            yc[d] = copy(mom.at[:, step4(y, d)], yx.at[y], {"y": step4(y, d)})

    def mom_swap():
        for d in (1, 3, 2):
            yc[d].wait_recv()
        for k in range(9):
            res = dot(perm64[...], yx[:, k].reshape(64, 1024)).astype(BF)
            for u in range(4):
                for h in range(2):
                    swp[k, u, h] = res[16 * u : 16 * u + 16, 512 * h : 512 * h + 512]
        n0, pending = deliver(0, lambda u, h: swp.at[:, u, h], fin.at[pl.ds(0, 9), z * 2 + c])
        msem[0] = n0
        late.extend(pending)

    def owned(k):
        return dot(perm128[...], fin[k].reshape(128, 512)).T

    def mom_land():
        landed(msem[0], 0, 9)
        for m in range(3):
            out_w[m] = owned(m)
            out_f[m] = owned(3 + m)
            out_s[m] = owned(6 + m)

    def update(m):
        landed(gsem[m], 9 + m, 1)
        grad = owned(9 + m)
        w = out_w[m]
        first = 0.9 * out_f[m] + 0.1 * grad
        second = 0.95 * out_s[m] + 0.05 * grad * grad
        out_f[m] = first
        out_s[m] = second
        out_w[m] = w - 8e-05 * (first / (jnp.sqrt(second) + 1e-08) + 0.1 * w)

    ag1(0)
    ag1(1)
    ag2(0)
    ag1(2)
    for k in (3, 4, 5):
        pack(k)
    xsend(3, 3)
    ag3(0)
    ag2(1)
    ag4(0)
    for k in (6, 7, 8):
        pack(k)
    xsend(6, 3)
    ag3(1)
    ag2(2)
    ag5(0)
    for d in tload[0::2]:
        d.wait()
    for d in mine:
        d.wait_recv()
    ag4(1)
    ag3(2)
    ag6(0)
    fwd(0)
    ag5(1)
    ag4(2)
    mom_pick(1)
    mom_pick(2)
    mom_y()
    ag6(1)
    fwd(1)
    ag5(2)
    gate = summed(0)
    up = summed(1)
    sig = 1.0 / (1.0 + jnp.exp(-gate))
    act = gate * sig
    share(2, act * up)
    for d in tload[1::2]:
        d.wait()
    for d in mine_cot:
        d.wait_recv()
    ag6(2)
    fwd(2)
    bwd(2)
    rs1(2)
    back = summed(2)
    share(0, back * up * (sig * (1.0 + gate * (1.0 - sig))))
    share(1, back * act)
    rs2(2)
    mom_swap()
    bwd(0)
    rs1(0)
    rs3(2)
    rs2(0)
    bwd(1)
    rs1(1)
    rs4(2)
    rs3(0)
    rs2(1)
    mom_land()
    rs5(2)
    rs4(0)
    rs3(1)
    rs5(0)
    update(2)
    rs4(1)
    update(0)
    rs5(1)
    update(1)
    for d in started:
        d.wait_send()
    for same, d in late:

        @pl.when(jnp.logical_not(same))
        def _():
            d.wait_send()


def on_device(old_weights, old_first, old_second, old_blocks, owner_map, inputs, cotangent):
    any_ = pl.BlockSpec(memory_space=pl.ANY)
    smem = pl.BlockSpec(memory_space=pltpu.SMEM)
    vmem = pl.BlockSpec(memory_space=pltpu.VMEM)
    V = pltpu.VMEM
    outs = pl.pallas_call(
        kernel,
        out_shape=[jax.ShapeDtypeStruct((3, 512, 128), F32)] * 3,
        in_specs=[smem, smem, any_, any_, any_, any_, any_],
        out_specs=[vmem] * 3,
        scratch_shapes=[
            V((9, 8, 16384), F32),
            V((9, 4, 16, 2048), BF),
            V((9, 4, 16, 2048), BF),
            V((9, 4, 16, 1024), BF),
            V((4, 9, 16, 1024), BF),
            V((9, 4, 2, 16, 512), BF),
            V((12, 8, 16, 512), BF),
            V((3, 4, 4, 16, 4096), BF),
            V((4, 256, 4096), BF),
            V((4, 256, 4096), BF),
            V((3, 4, 256, 256), BF),
            V((3, 3, 256, 256), BF),
            V((3, 4, 256, 256), BF),
            V((3, 2, 4, 4, 64, 512), BF),
            V((3, 2, 2, 2, 64, 512), BF),
            V((3, 2, 2, 4, 64, 512), BF),
            V((3, 2, 4, 64, 512), BF),
            V((3, 2, 2, 32, 512), BF),
            V((3, 2, 2, 64, 512), BF),
            V((3, 2, 4, 16, 512), BF),
            V((16, 64), BF),
            V((16, 64), BF),
            V((256, 256), BF),
            V((64, 64), BF),
            V((128, 128), BF),
            pltpu.SemaphoreType.DMA((NS,)),
            pltpu.SemaphoreType.DMA((NS,)),
            pltpu.SemaphoreType.DMA((16,)),
        ],
        compiler_params=pltpu.CompilerParams(
            collective_id=0, has_side_effects=True, vmem_limit_bytes=64 * 1024 * 1024
        ),
        name="restore_step",
    )(
        old_blocks, owner_map.T, old_weights, old_first, old_second,
        inputs.reshape(480, 4096), cotangent.reshape(480, 16384),
    )
    return tuple(jnp.transpose(o, (1, 0, 2)) for o in outs)


def solution(mesh):
    grid = Mesh(mesh.devices.reshape(4, 4, 2, 4), ("z", "y", "c", "x"))
    dp = ("z", "y", "c")
    shard = P(None, ("z", "y", "c", "x"), None)
    in_specs = (shard, shard, shard, P(), P(), P(None, dp, "x"), P(None, dp, None))
    out_specs = (P(dp, None, "x"),) * 3
    return jax.shard_map(
        on_device, mesh=grid, in_specs=in_specs, out_specs=out_specs, check_vma=False
    )
```

```python
import functools

import jax
import jax.numpy as jnp
from jax import lax
from jax.experimental import pallas as pl
from jax.experimental.pallas import tpu as pltpu
from jax.sharding import Mesh, PartitionSpec as P

BF = jnp.bfloat16
F32 = jnp.float32
MESH = pl.DeviceIdType.MESH
NS = 320


def dot_nt(a, b):
    return lax.dot_general(a, b, (((1,), (1,)), ((), ())), preferred_element_type=F32)


def dot(a, b):
    return jnp.dot(a, b, preferred_element_type=F32)


def iota(shape, dim):
    return lax.broadcasted_iota(jnp.int32, shape, dim)


def kernel(
    blocks, owners, old_w, old_f, old_s, tok_in, cot_in,
    out,
    stage, xs, xr, mom, yx, swp, fin, wall, tok, cot, part, part_in, sgr, grd, r1, r2, ysum, r4, zed,
    sel_a, sel_b, perm, perm64, perm128,
    ssem, rsem, lsem, gsum,
):
    z, y, c, x = (lax.axis_index(a) for a in ("z", "y", "c", "x"))
    step4 = lambda v, d: lax.rem(v + d + 4, 4)
    counter = [0]
    started = []

    def copy(src, dst, dev):
        n = counter[0]
        counter[0] += 1
        d = pltpu.make_async_remote_copy(
            src_ref=src, dst_ref=dst, send_sem=ssem.at[n], recv_sem=rsem.at[n],
            device_id=dev, device_id_type=MESH,
        )
        d.start()
        started.append(d)
        return d

    barrier = pltpu.get_barrier_semaphore()

    def greet(dev):
        pl.semaphore_signal(barrier, inc=1, device_id=dev, device_id_type=MESH)

    for d in (1, 2, 3):
        greet({"x": step4(x, d)})
        greet({"y": step4(y, d)})
    for d in (1, 3):
        greet({"z": step4(z, d)})
    greet({"c": 1 - c})
    for zs in range(4):
        for cs in range(2):
            greet({"x": z, "z": zs, "c": cs})

    olds = (old_w, old_f, old_s)
    local = []

    def load(src, dst):
        d = pltpu.make_async_copy(src, dst, lsem.at[len(local)])
        d.start()
        local.append(d)
        return d

    loads = [load(olds[k // 3].at[k % 3], stage.at[k]) for k in range(9)]
    quarter = pl.ds(pl.multiple_of(x * 4096, 4096), 4096)
    tload = []
    for mb in range(2):
        rows = pl.ds(240 * mb, 240)
        tload.append(load(tok_in.at[rows], tok.at[2 * c + mb, pl.ds(0, 240)]))
        tload.append(load(cot_in.at[rows, quarter], cot.at[2 * c + mb, pl.ds(0, 240)]))
    tok[:, 240:, :] = jnp.zeros((4, 16, 4096), BF)
    cot[:, 240:, :] = jnp.zeros((4, 16, 4096), BF)

    shape = (16, 64)
    row, col = iota(shape, 0), iota(shape, 1)
    ru, ri = row // 4, row % 4
    cx, ch, cj, cs = col // 16, (col // 8) % 2, (col // 4) % 2, col % 4
    dp = z * 8 + y * 2 + c
    group = jnp.full(shape, -1, jnp.int32)
    for xx in range(4):
        held = blocks[dp * 4 + xx]
        base = 2 * (xx // 2) + (blocks[dp * 4 + xx - 1] if xx % 2 else 0)
        for j in range(2):
            group = jnp.where((cx == xx) & (cj == j), jnp.where(j < held, base + j, -1), group)
    who = jnp.full(shape, -1, jnp.int32)
    for i in range(4):
        for s in range(4):
            who = jnp.where((ri == i) & (cs == s), owners[s, dp * 4 + i], who)
    hit = (group == ri) & (who == ru)
    sel_a[...] = jnp.where(hit & (ch == 0), 1.0, 0.0).astype(BF)
    sel_b[...] = jnp.where(hit & (ch == 1), 1.0, 0.0).astype(BF)
    r, q = iota((64, 64), 0), iota((64, 64), 1)
    want = ((r // 4) % 4) * 16 + (r // 16) * 4 + r % 4
    perm64[...] = jnp.where(q == want, 1.0, 0.0).astype(BF)
    r, q = iota((256, 256), 0), iota((256, 256), 1)
    want = (r // 64) * 64 + ((r // 4) % 4) * 16 + ((r // 16) % 4) * 4 + r % 4
    perm[...] = jnp.where(q == want, 1.0, 0.0).astype(BF)
    r, q = iota((128, 128), 0), iota((128, 128), 1)
    want = (r // 32) * 32 + ((r // 4) % 2) * 16 + ((r // 8) % 4) * 4 + r % 4
    perm128[...] = jnp.where(q == want, 1.0, 0.0).astype(BF)

    def pack(k):
        loads[k].wait()
        for xx in range(4):
            lo = stage[k, :, xx * 4096 : xx * 4096 + 2048]
            hi = stage[k, :, xx * 4096 + 2048 : xx * 4096 + 4096]
            xs[k, xx] = jnp.concatenate([lo, hi], axis=0).astype(BF)
        xr[k, x] = xs[k, x]

    pack(0)
    pl.semaphore_wait(barrier, 17)

    xcop = {}

    def xsend(k, n):
        ks = pl.ds(k, n)
        for d in (1, 3, 2):
            xcop[k, d] = copy(xs.at[ks, step4(x, d)], xr.at[ks, x], {"x": step4(x, d)})

    xsend(0, 1)
    sib = {"c": 1 - c}
    mine, mine_cot = [], []
    for mb in range(2):
        rows = pl.ds(240 * mb, 240)
        mine.append(copy(tok_in.at[rows], tok.at[2 * c + mb, pl.ds(0, 240)], sib))
    for mb in range(2):
        rows = pl.ds(240 * mb, 240)
        mine_cot.append(copy(cot_in.at[rows, quarter], cot.at[2 * c + mb, pl.ds(0, 240)], sib))

    def xwait(k):
        for d in (1, 3, 2):
            xcop[k, d].wait_recv()

    def select(k):
        rows = xr[k].reshape(64, 2048)
        return dot(sel_a[...], rows).astype(BF), dot(sel_b[...], rows).astype(BF)

    def wref(m, h, first, second, lo, n):
        cols = pl.ds(2048 * h + lo, n)
        if h == 0:
            return wall.at[m, second, first, :, cols]
        return wall.at[m, first, second, :, cols]

    def ring1(h, d):
        return {"y": step4(y, d)} if h == 0 else {"z": step4(z, d)}

    def ring2(h, d):
        return {"z": step4(z, d)} if h == 0 else {"y": step4(y, d)}

    def at1(h, d):
        return step4(y if h == 0 else z, d)

    def at2(h, d):
        return step4(z if h == 0 else y, d)

    ag = {}
    ITEM = (0, -1, 1, 2)

    def out2(m, h, j):
        piece = wref(m, h, at1(h, ITEM[j]), at2(h, 0), 0, 2048)
        ag[m, h, j, "l"] = copy(piece, piece, ring2(h, 1))
        ag[m, h, j, "r"] = copy(piece, piece, ring2(h, -1))

    def pack_w(m):
        pack(m)
        xsend(m, 1)

    def ag1(m):
        xwait(m)
        a, b = select(m)
        wall[m, z, y, :, 0:2048] = a
        wall[m, z, y, :, 2048:4096] = b
        for h in range(2):
            piece = wref(m, h, at1(h, 0), at2(h, 0), 0, 2048)
            ag[m, h, "l"] = copy(piece, piece, ring1(h, 1))
            ag[m, h, "r"] = copy(piece, piece, ring1(h, -1))
        for h in range(2):
            out2(m, h, 0)

    def ag2(m, h, j):
        if j == 1:
            ag[m, h, "l"].wait_recv()
            piece = wref(m, h, at1(h, -1), at2(h, 0), 0, 1024)
            ag[m, h, "fl"] = copy(piece, piece, ring1(h, 1))
        elif j == 2:
            ag[m, h, "r"].wait_recv()
            piece = wref(m, h, at1(h, 1), at2(h, 0), 1024, 1024)
            ag[m, h, "fr"] = copy(piece, piece, ring1(h, -1))
        else:
            ag[m, h, "fl"].wait_recv()
            ag[m, h, "fr"].wait_recv()
        out2(m, h, j)

    def fw(m, h, j):
        ag[m, h, j, "l"].wait_recv()
        piece = wref(m, h, at1(h, ITEM[j]), at2(h, -1), 0, 1024)
        ag[m, h, j, "fl"] = copy(piece, piece, ring2(h, 1))
        ag[m, h, j, "r"].wait_recv()
        piece = wref(m, h, at1(h, ITEM[j]), at2(h, 1), 1024, 1024)
        ag[m, h, j, "fr"] = copy(piece, piece, ring2(h, -1))

    pc = {}
    ready = set()

    def acts_of(m):
        n = 1 if m == 2 else 0
        if n not in ready:
            ready.add(n)
            for d in tload[n::2]:
                d.wait()
            for d in (mine, mine_cot)[n]:
                d.wait_recv()
        return (tok, cot)[n]

    def fwd(m):
        acts = acts_of(m)
        for h in range(2):
            for j in range(4):
                ag[m, h, j, "fl"].wait_recv()
                ag[m, h, j, "fr"].wait_recv()

        def body(b, carry):
            part[m, b] = dot_nt(acts[b], wall[m].reshape(256, 4096)).astype(BF)
            return carry

        lax.fori_loop(0, 4, body, 0)
        rows = pl.ds(0, 240)
        for d in (1, 3, 2):
            pc[m, d] = copy(
                part.at[m, step4(x, d), rows], part_in.at[m, d - 1, rows], {"x": step4(x, d)}
            )

    def summed(m):
        for d in (1, 3, 2):
            pc[m, d].wait_recv()
        total = part[m, x].astype(F32)
        for d in range(3):
            total = total + part_in[m, d].astype(F32)
        return total

    sc = {}

    def share(m, value):
        sgr[m, x] = dot_nt(perm[...], value.astype(BF)).astype(BF)
        for d in (1, 3, 2):
            sc[m, d] = copy(sgr.at[m, x], sgr.at[m, x], {"x": step4(x, d)})

    kept = {}

    def hid():
        gate = summed(0)
        up = summed(1)
        sig = 1.0 / (1.0 + jnp.exp(-gate))
        act = gate * sig
        kept["act"] = act
        kept["slope"] = up * (sig * (1.0 + gate * (1.0 - sig)))
        share(2, act * up)

    def dg(m):
        if "back" not in kept:
            kept["back"] = summed(2)
        share(m, kept["back"] * kept["slope" if m == 0 else "act"])

    rs = {}

    def bwd(m):
        acts = acts_of(m)
        for d in (1, 3, 2):
            sc[m, d].wait_recv()

        def body(n, carry):
            cols = pl.ds(pl.multiple_of(n * 512, 512), 512)
            left = jnp.concatenate([sgr[m, b] for b in range(4)], axis=1)
            right = acts[:, :, cols].reshape(1024, 512)
            res = dot(left, right).astype(BF).reshape(4, 64, 512)
            grd[m, lax.rem(n, 2), n // 2] = res
            return carry

        lax.fori_loop(0, 8, body, 0)
        for h in range(2):
            far = at2(h, 2)
            for half in range(2):
                if h == 0:
                    src = grd.at[m, h, pl.ds(2 * half, 2), far]
                else:
                    src = grd.at[m, h, far, pl.ds(2 * half, 2)]
                rs[m, h, 1, half] = copy(src, r1.at[m, h, half], ring2(h, 1 if half == 0 else -1))

    def gref(m, h, p, q):
        return (m, h, q, p) if h == 0 else (m, h, p, q)

    def rs2(m, h):
        for half in range(2):
            rs[m, h, 1, half].wait_recv()
            to = 1 if half == 0 else -1
            p = at2(h, to)
            for k in range(2):
                at = gref(m, h, p, 2 * half + k)
                grd[at] = (grd[at].astype(F32) + r1[m, h, half, k].astype(F32)).astype(BF)
            src = grd.at[m, h, :, p] if h == 0 else grd.at[m, h, p]
            rs[m, h, 2, half] = copy(src, r2.at[m, h, half], ring2(h, to))

    def rs3(m, h):
        rs[m, h, 2, 0].wait_recv()
        rs[m, h, 2, 1].wait_recv()
        for q in range(4):
            own = grd[gref(m, h, at2(h, 0), q)].astype(F32)
            ysum[m, h, q] = (
                own + r2[m, h, 0, q].astype(F32) + r2[m, h, 1, q].astype(F32)
            ).astype(BF)
        for d in (2, 1, 3):
            rs[m, h, 4, d] = copy(ysum.at[m, h, at1(h, d)], r4.at[m, h, d - 1], ring1(h, d))

    def deliver(ref_of, dst):
        n0 = counter[0]
        counter[0] += 8
        for u in range(4):
            for h in range(2):
                same = (x == z) & (x == u) & (c == h)
                remote = pltpu.make_async_remote_copy(
                    src_ref=ref_of(u, h), dst_ref=dst, send_sem=ssem.at[n0 + u * 2 + h],
                    recv_sem=rsem.at[n0], device_id={"x": u, "z": x, "c": h}, device_id_type=MESH,
                )
                late.append((same, remote))

                @pl.when(jnp.logical_not(same))
                def _():
                    remote.start()

                @pl.when(same)
                def _():
                    pltpu.make_async_copy(ref_of(u, h), dst, rsem.at[n0]).start()

        return n0

    late = []
    gsem = {}
    msem = {}

    def rs5(m, h):
        for d in (1, 3, 2):
            rs[m, h, 4, d].wait_recv()
        own = ysum[m, h, at1(h, 0)].astype(F32)
        for d in range(3):
            own = own + r4[m, h, d].astype(F32)
        zed[m, h] = own.astype(BF).reshape(4, 16, 512)
        n0 = counter[0]
        counter[0] += 4
        gsem.setdefault(m, {})[h] = n0
        for u in range(4):
            same = (x == z) & (x == u) & (c == h)
            src, dst = zed.at[m, h, u], fin.at[9 + m, z * 2 + c]
            remote = pltpu.make_async_remote_copy(
                src_ref=src, dst_ref=dst, send_sem=ssem.at[n0 + u],
                recv_sem=gsum.at[m], device_id={"x": u, "z": x, "c": h}, device_id_type=MESH,
            )
            late.append((same, remote))

            @pl.when(jnp.logical_not(same))
            def _():
                remote.start()

            @pl.when(same)
            def _():
                pltpu.make_async_copy(src, dst, gsum.at[m]).start()

    def landed(sem, k, n):
        whole = fin.at[pl.ds(k, n)]
        pltpu.make_async_copy(whole, whole, sem).wait()

    yc = {}

    def mpack(a):
        for k in range(3 * a, 3 * a + 3):
            pack(k)
        xsend(3 * a, 3)

    def mpick(a):
        xwait(3 * a)
        ks = pl.ds(3 * a, 3)
        for k in range(3 * a, 3 * a + 3):
            lo, hi = select(k)
            for yy in range(4):
                half = lo if yy < 2 else hi
                mom[k, yy] = half[:, 1024 * (yy % 2) : 1024 * (yy % 2) + 1024]
        yx[y, ks] = mom[ks, y]
        for d in (1, 3, 2):
            yc[a, d] = copy(mom.at[ks, step4(y, d)], yx.at[y, ks], {"y": step4(y, d)})

    def mswap(a):
        if a:
            for d in (1, 3, 2):
                yc[a, d].wait_recv()
        for k in range(3 * a, 3 * a + 3):
            if a:
                rows = yx[:, k].reshape(64, 1024)
            else:
                cols = pl.ds(pl.multiple_of(y * 1024, 1024), 1024)
                rows = wall[k, z, :, :, cols].reshape(64, 1024)
            res = dot(perm64[...], rows).astype(BF)
            for u in range(4):
                for h in range(2):
                    swp[k, u, h] = res[16 * u : 16 * u + 16, 512 * h : 512 * h + 512]
        ks = pl.ds(3 * a, 3)
        msem[a] = deliver(lambda u, h: swp.at[ks, u, h], fin.at[ks, z * 2 + c])

    def owned(k):
        out[k] = dot(perm128[...], fin[k].reshape(128, 512)).T.astype(BF)

    def mland(a):
        landed(rsem.at[msem[a]], 3 * a, 3)
        for k in range(3 * a, 3 * a + 3):
            owned(k)

    def upd(m):
        landed(gsum.at[m], 9 + m, 1)
        owned(9 + m)

    part_in[:, :, 240:, :] = jnp.zeros((3, 3, 16, 256), BF)
    pack_w(1)
    ag1(0)
    mpack(2)
    ag1(1)
    ag2(1, 0, 1)
    ag2(1, 0, 2)
    ag2(1, 1, 2)
    ag2(1, 1, 1)
    pack_w(2)
    ag2(0, 1, 1)
    fw(1, 0, 0)
    ag2(0, 0, 1)
    ag2(0, 0, 2)
    ag2(1, 1, 3)
    fw(1, 0, 2)
    ag2(1, 0, 3)
    fw(1, 1, 1)
    mpack(1)
    fw(0, 1, 1)
    fw(1, 1, 3)
    fw(1, 1, 0)
    ag2(0, 1, 2)
    fw(1, 1, 2)
    ag2(0, 0, 3)
    fw(1, 0, 3)
    fw(1, 0, 1)
    fw(0, 0, 2)
    fw(0, 0, 0)
    ag2(0, 1, 3)
    fw(0, 0, 1)
    fw(0, 1, 0)
    ag1(2)
    fwd(1)
    fw(0, 0, 3)
    fw(0, 1, 2)
    fw(0, 1, 3)
    ag2(2, 0, 1)
    ag2(2, 0, 2)
    ag2(2, 1, 2)
    mpick(2)
    ag2(2, 1, 1)
    fwd(0)
    fw(2, 1, 0)
    fw(2, 0, 1)
    fw(2, 0, 0)
    ag2(2, 1, 3)
    ag2(2, 0, 3)
    mswap(2)
    fw(2, 1, 3)
    fw(2, 0, 3)
    hid()
    fw(2, 1, 1)
    fw(2, 1, 2)
    fw(2, 0, 2)
    fwd(2)
    mswap(0)
    mpick(1)
    bwd(2)
    dg(1)
    rs2(2, 0)
    rs2(2, 1)
    dg(0)
    mswap(1)
    bwd(1)
    rs3(2, 0)
    mland(2)
    rs3(2, 1)
    bwd(0)
    rs2(1, 1)
    rs2(1, 0)
    mland(1)
    rs5(2, 1)
    mland(0)
    rs5(2, 0)
    rs2(0, 1)
    rs2(0, 0)
    rs3(1, 0)
    rs3(1, 1)
    rs3(0, 1)
    rs3(0, 0)
    rs5(1, 0)
    upd(2)
    rs5(1, 1)
    rs5(0, 0)
    rs5(0, 1)
    upd(1)
    upd(0)
    for d in started:
        d.wait_send()
    for same, d in late:

        @pl.when(jnp.logical_not(same))
        def _():
            d.wait_send()


def on_device(old_weights, old_first, old_second, old_blocks, owner_map, inputs, cotangent):
    any_ = pl.BlockSpec(memory_space=pl.ANY)
    smem = pl.BlockSpec(memory_space=pltpu.SMEM)
    vmem = pl.BlockSpec(memory_space=pltpu.VMEM)
    V = pltpu.VMEM
    states = pl.pallas_call(
        kernel,
        out_shape=jax.ShapeDtypeStruct((12, 512, 128), BF),
        in_specs=[smem, smem, any_, any_, any_, any_, any_],
        out_specs=vmem,
        scratch_shapes=[
            V((9, 8, 16384), F32),
            V((9, 4, 16, 2048), BF),
            V((9, 4, 16, 2048), BF),
            V((9, 4, 16, 1024), BF),
            V((4, 9, 16, 1024), BF),
            V((9, 4, 2, 16, 512), BF),
            V((12, 8, 16, 512), BF),
            V((3, 4, 4, 16, 4096), BF),
            V((4, 256, 4096), BF),
            V((4, 256, 4096), BF),
            V((3, 4, 256, 256), BF),
            V((3, 3, 256, 256), BF),
            V((3, 4, 256, 256), BF),
            V((3, 2, 4, 4, 64, 512), BF),
            V((3, 2, 2, 2, 64, 512), BF),
            V((3, 2, 2, 4, 64, 512), BF),
            V((3, 2, 4, 64, 512), BF),
            V((3, 2, 3, 64, 512), BF),
            V((3, 2, 4, 16, 512), BF),
            V((16, 64), BF),
            V((16, 64), BF),
            V((256, 256), BF),
            V((64, 64), BF),
            V((128, 128), BF),
            pltpu.SemaphoreType.DMA((NS,)),
            pltpu.SemaphoreType.DMA((NS,)),
            pltpu.SemaphoreType.DMA((16,)),
            pltpu.SemaphoreType.DMA((3,)),
        ],
        compiler_params=pltpu.CompilerParams(
            collective_id=0, has_side_effects=True, vmem_limit_bytes=64 * 1024 * 1024
        ),
        name="restore_step",
    )(
        old_blocks, owner_map.T, old_weights, old_first, old_second,
        inputs.reshape(480, 4096), cotangent.reshape(480, 16384),
    )
    w, first, second, grad = (states[3 * i : 3 * i + 3].astype(F32) for i in range(4))
    first = 0.9 * first + 0.1 * grad
    second = 0.95 * second + 0.05 * grad * grad
    w = w - 8e-05 * (first / (jnp.sqrt(second) + 1e-08) + 0.1 * w)
    return tuple(jnp.transpose(o, (1, 0, 2)) for o in (w, first, second))


def solution(mesh):
    grid = Mesh(mesh.devices.reshape(4, 4, 2, 4), ("z", "y", "c", "x"))
    dp = ("z", "y", "c")
    shard = P(None, ("z", "y", "c", "x"), None)
    in_specs = (shard, shard, shard, P(), P(), P(None, dp, "x"), P(None, dp, None))
    out_specs = (P(dp, None, "x"),) * 3
    return jax.shard_map(
        on_device, mesh=grid, in_specs=in_specs, out_specs=out_specs, check_vma=False
    )
```

```python
import functools

import jax
import jax.numpy as jnp
from jax import lax
from jax.experimental import pallas as pl
from jax.experimental.pallas import tpu as pltpu
from jax.sharding import Mesh, PartitionSpec as P

BF = jnp.bfloat16
F32 = jnp.float32
MESH = pl.DeviceIdType.MESH
NS = 400


def dot_nt(a, b):
    return lax.dot_general(a, b, (((1,), (1,)), ((), ())), preferred_element_type=F32)


def dot(a, b):
    return jnp.dot(a, b, preferred_element_type=F32)


def iota(shape, dim):
    return lax.broadcasted_iota(jnp.int32, shape, dim)


def kernel(
    blocks, owners, old_w, old_f, old_s, tok_in, cot_in,
    out,
    stage, xs, xr, mom, yx, swp, fin, wall, tok, cot, part, part_in, sgr, grd, r1, r2, ysum, r4, zed,
    sel_a, sel_b, perm, perm64, perm128,
    ssem, rsem, lsem, gsum,
):
    z, y, c, x = (lax.axis_index(a) for a in ("z", "y", "c", "x"))
    step4 = lambda v, d: lax.rem(v + d + 4, 4)
    counter = [0]
    started = []

    def copy(src, dst, dev):
        n = counter[0]
        counter[0] += 1
        d = pltpu.make_async_remote_copy(
            src_ref=src, dst_ref=dst, send_sem=ssem.at[n], recv_sem=rsem.at[n],
            device_id=dev, device_id_type=MESH,
        )
        d.start()
        started.append(d)
        return d

    barrier = pltpu.get_barrier_semaphore()

    def greet(dev):
        pl.semaphore_signal(barrier, inc=1, device_id=dev, device_id_type=MESH)

    for d in (1, 2, 3):
        greet({"x": step4(x, d)})
        greet({"y": step4(y, d)})
    for d in (1, 3):
        greet({"z": step4(z, d)})
    greet({"c": 1 - c})
    for zs in range(4):
        for cs in range(2):
            greet({"x": z, "z": zs, "c": cs})

    olds = (old_w, old_f, old_s)
    local = []

    def load(src, dst):
        d = pltpu.make_async_copy(src, dst, lsem.at[len(local)])
        d.start()
        local.append(d)
        return d

    loads = [load(olds[k // 3].at[k % 3], stage.at[k]) for k in range(9)]
    quarter = pl.ds(pl.multiple_of(x * 4096, 4096), 4096)
    tload = []
    for mb in range(2):
        rows = pl.ds(240 * mb, 240)
        tload.append(load(tok_in.at[rows], tok.at[2 * c + mb, pl.ds(0, 240)]))
        tload.append(load(cot_in.at[rows, quarter], cot.at[2 * c + mb, pl.ds(0, 240)]))
    tok[:, 240:, :] = jnp.zeros((4, 16, 4096), BF)
    cot[:, 240:, :] = jnp.zeros((4, 16, 4096), BF)

    shape = (16, 64)
    row, col = iota(shape, 0), iota(shape, 1)
    ru, ri = row // 4, row % 4
    cx, ch, cj, cs = col // 16, (col // 8) % 2, (col // 4) % 2, col % 4
    dp = z * 8 + y * 2 + c
    group = jnp.full(shape, -1, jnp.int32)
    for xx in range(4):
        held = blocks[dp * 4 + xx]
        base = 2 * (xx // 2) + (blocks[dp * 4 + xx - 1] if xx % 2 else 0)
        for j in range(2):
            group = jnp.where((cx == xx) & (cj == j), jnp.where(j < held, base + j, -1), group)
    who = jnp.full(shape, -1, jnp.int32)
    for i in range(4):
        for s in range(4):
            who = jnp.where((ri == i) & (cs == s), owners[s, dp * 4 + i], who)
    hit = (group == ri) & (who == ru)
    sel_a[...] = jnp.where(hit & (ch == 0), 1.0, 0.0).astype(BF)
    sel_b[...] = jnp.where(hit & (ch == 1), 1.0, 0.0).astype(BF)
    r, q = iota((64, 64), 0), iota((64, 64), 1)
    want = ((r // 4) % 4) * 16 + (r // 16) * 4 + r % 4
    perm64[...] = jnp.where(q == want, 1.0, 0.0).astype(BF)
    r, q = iota((256, 256), 0), iota((256, 256), 1)
    want = (r // 64) * 64 + ((r // 4) % 4) * 16 + ((r // 16) % 4) * 4 + r % 4
    perm[...] = jnp.where(q == want, 1.0, 0.0).astype(BF)
    r, q = iota((128, 128), 0), iota((128, 128), 1)
    want = (r // 32) * 32 + ((r // 4) % 2) * 16 + ((r // 8) % 4) * 4 + r % 4
    perm128[...] = jnp.where(q == want, 1.0, 0.0).astype(BF)

    def pack(k):
        loads[k].wait()
        for xx in range(4):
            lo = stage[k, :, xx * 4096 : xx * 4096 + 2048]
            hi = stage[k, :, xx * 4096 + 2048 : xx * 4096 + 4096]
            xs[k, xx] = jnp.concatenate([lo, hi], axis=0).astype(BF)
        xr[k, x] = xs[k, x]

    pack(0)
    pl.semaphore_wait(barrier, 17)

    xcop = {}

    def xsend(k, n):
        ks = pl.ds(k, n)
        for d in (1, 3, 2):
            xcop[k, d] = copy(xs.at[ks, step4(x, d)], xr.at[ks, x], {"x": step4(x, d)})

    xsend(0, 1)
    sib = {"c": 1 - c}
    mine, mine_cot = [], []
    for mb in range(2):
        rows = pl.ds(240 * mb, 240)
        mine.append(copy(tok_in.at[rows], tok.at[2 * c + mb, pl.ds(0, 240)], sib))
    for mb in range(2):
        rows = pl.ds(240 * mb, 240)
        mine_cot.append(copy(cot_in.at[rows, quarter], cot.at[2 * c + mb, pl.ds(0, 240)], sib))

    def xwait(k):
        for d in (1, 3, 2):
            xcop[k, d].wait_recv()

    def select(k):
        rows = xr[k].reshape(64, 2048)
        return dot(sel_a[...], rows).astype(BF), dot(sel_b[...], rows).astype(BF)

    def wref(m, h, first, second, lo, n):
        cols = pl.ds(2048 * h + lo, n)
        if h == 0:
            return wall.at[m, second, first, :, cols]
        return wall.at[m, first, second, :, cols]

    def ring1(h, d):
        return {"y": step4(y, d)} if h == 0 else {"z": step4(z, d)}

    def ring2(h, d):
        return {"z": step4(z, d)} if h == 0 else {"y": step4(y, d)}

    def at1(h, d):
        return step4(y if h == 0 else z, d)

    def at2(h, d):
        return step4(z if h == 0 else y, d)

    ag = {}
    ITEM = (0, -1, 1, 2)

    def out2(m, h, j):
        piece = wref(m, h, at1(h, ITEM[j]), at2(h, 0), 0, 2048)
        ag[m, h, j, "l"] = copy(piece, piece, ring2(h, 1))
        ag[m, h, j, "r"] = copy(piece, piece, ring2(h, -1))

    def pack_w(m):
        pack(m)
        xsend(m, 1)

    def ag1(m):
        xwait(m)
        a, b = select(m)
        wall[m, z, y, :, 0:2048] = a
        wall[m, z, y, :, 2048:4096] = b
        for h in range(2):
            piece = wref(m, h, at1(h, 0), at2(h, 0), 0, 2048)
            ag[m, h, "l"] = copy(piece, piece, ring1(h, 1))
            ag[m, h, "r"] = copy(piece, piece, ring1(h, -1))
        for h in range(2):
            piece = wref(m, h, at1(h, 0), at2(h, 0), 0, 2048)
            ag[m, h, "o"] = copy(piece, piece, ring1(h, 2))
        for h in range(2):
            out2(m, h, 0)

    def ag2(m, h, j):
        ag[m, h, (None, "l", "r", "o")[j]].wait_recv()
        out2(m, h, j)

    def fw(m, h, j):
        ag[m, h, j, "l"].wait_recv()
        piece = wref(m, h, at1(h, ITEM[j]), at2(h, -1), 0, 1024)
        ag[m, h, j, "fl"] = copy(piece, piece, ring2(h, 1))
        ag[m, h, j, "r"].wait_recv()
        piece = wref(m, h, at1(h, ITEM[j]), at2(h, 1), 1024, 1024)
        ag[m, h, j, "fr"] = copy(piece, piece, ring2(h, -1))

    pc = {}
    ready = set()

    def acts_of(m):
        n = 1 if m == 2 else 0
        if n not in ready:
            ready.add(n)
            for d in tload[n::2]:
                d.wait()
            for d in (mine, mine_cot)[n]:
                d.wait_recv()
        return (tok, cot)[n]

    def fwd(m):
        acts = acts_of(m)
        for h in range(2):
            for j in range(4):
                ag[m, h, j, "fl"].wait_recv()
                ag[m, h, j, "fr"].wait_recv()

        n0 = counter[0]
        counter[0] += 3
        rows = pl.ds(0, 240)

        def piece(d, n):
            b = step4(x, d)
            return pltpu.make_async_remote_copy(
                src_ref=part.at[m, b, rows], dst_ref=part_in.at[m, d - 1, rows],
                send_sem=ssem.at[n], recv_sem=rsem.at[n],
                device_id={"x": b}, device_id_type=MESH,
            )

        def body(i, carry):
            b = step4(x, i + 1)
            part[m, b] = dot_nt(acts[b], wall[m].reshape(256, 4096)).astype(BF)

            @pl.when(i < 3)
            def _():
                piece(i + 1, n0 + i).start()

            return carry

        lax.fori_loop(0, 4, body, 0)
        for d in (1, 2, 3):
            pc[m, d] = piece(d, n0 + d - 1)
            started.append(pc[m, d])

    def summed(m):
        for d in (1, 3, 2):
            pc[m, d].wait_recv()
        total = part[m, x].astype(F32)
        for d in range(3):
            total = total + part_in[m, d].astype(F32)
        return total

    sc = {}

    def share(m, value):
        sgr[m, x] = dot_nt(perm[...], value.astype(BF)).astype(BF)
        for d in (1, 3, 2):
            sc[m, d] = copy(sgr.at[m, x], sgr.at[m, x], {"x": step4(x, d)})

    kept = {}

    def hid():
        gate = summed(0)
        up = summed(1)
        sig = 1.0 / (1.0 + jnp.exp(-gate))
        act = gate * sig
        kept["act"] = act
        kept["slope"] = up * (sig * (1.0 + gate * (1.0 - sig)))
        share(2, act * up)

    def dg(m):
        if "back" not in kept:
            kept["back"] = summed(2)
        share(m, kept["back"] * kept["slope" if m == 0 else "act"])

    rs = {}

    def bwd(m):
        acts = acts_of(m)
        for d in (1, 3, 2):
            sc[m, d].wait_recv()

        def body(n, carry):
            cols = pl.ds(pl.multiple_of(n * 512, 512), 512)
            left = jnp.concatenate([sgr[m, b] for b in range(4)], axis=1)
            right = acts[:, :, cols].reshape(1024, 512)
            res = dot(left, right).astype(BF).reshape(4, 64, 512)
            grd[m, lax.rem(n, 2), n // 2] = res
            return carry

        lax.fori_loop(0, 8, body, 0)
        for h in range(2):
            far = at2(h, 2)
            for half in range(2):
                if h == 0:
                    src = grd.at[m, h, pl.ds(2 * half, 2), far]
                else:
                    src = grd.at[m, h, far, pl.ds(2 * half, 2)]
                rs[m, h, 1, half] = copy(src, r1.at[m, h, half], ring2(h, 1 if half == 0 else -1))

    def gref(m, h, p, q):
        return (m, h, q, p) if h == 0 else (m, h, p, q)

    def rs2(m, h):
        for half in range(2):
            rs[m, h, 1, half].wait_recv()
            to = 1 if half == 0 else -1
            p = at2(h, to)
            for k in range(2):
                at = gref(m, h, p, 2 * half + k)
                grd[at] = (grd[at].astype(F32) + r1[m, h, half, k].astype(F32)).astype(BF)
            src = grd.at[m, h, :, p] if h == 0 else grd.at[m, h, p]
            rs[m, h, 2, half] = copy(src, r2.at[m, h, half], ring2(h, to))

    def rs3(m, h):
        rs[m, h, 2, 0].wait_recv()
        rs[m, h, 2, 1].wait_recv()
        for q in range(4):
            own = grd[gref(m, h, at2(h, 0), q)].astype(F32)
            ysum[m, h, q] = (
                own + r2[m, h, 0, q].astype(F32) + r2[m, h, 1, q].astype(F32)
            ).astype(BF)
        for d in (2, 1, 3):
            rs[m, h, 4, d] = copy(ysum.at[m, h, at1(h, d)], r4.at[m, h, d - 1], ring1(h, d))

    def deliver(ref_of, dst):
        n0 = counter[0]
        counter[0] += 8
        for u in range(4):
            for h in range(2):
                same = (x == z) & (x == u) & (c == h)
                remote = pltpu.make_async_remote_copy(
                    src_ref=ref_of(u, h), dst_ref=dst, send_sem=ssem.at[n0 + u * 2 + h],
                    recv_sem=rsem.at[n0], device_id={"x": u, "z": x, "c": h}, device_id_type=MESH,
                )
                late.append((same, remote))

                @pl.when(jnp.logical_not(same))
                def _():
                    remote.start()

                @pl.when(same)
                def _():
                    pltpu.make_async_copy(ref_of(u, h), dst, rsem.at[n0]).start()

        return n0

    late = []
    gsem = {}
    msem = {}

    def rs5(m, h):
        for d in (1, 3, 2):
            rs[m, h, 4, d].wait_recv()
        own = ysum[m, h, at1(h, 0)].astype(F32)
        for d in range(3):
            own = own + r4[m, h, d].astype(F32)
        zed[m, h] = own.astype(BF).reshape(4, 16, 512)
        n0 = counter[0]
        counter[0] += 4
        gsem.setdefault(m, {})[h] = n0
        for u in range(4):
            same = (x == z) & (x == u) & (c == h)
            src, dst = zed.at[m, h, u], fin.at[9 + m, z * 2 + c]
            remote = pltpu.make_async_remote_copy(
                src_ref=src, dst_ref=dst, send_sem=ssem.at[n0 + u],
                recv_sem=gsum.at[m], device_id={"x": u, "z": x, "c": h}, device_id_type=MESH,
            )
            late.append((same, remote))

            @pl.when(jnp.logical_not(same))
            def _():
                remote.start()

            @pl.when(same)
            def _():
                pltpu.make_async_copy(src, dst, gsum.at[m]).start()

    def landed(sem, k, n):
        whole = fin.at[pl.ds(k, n)]
        pltpu.make_async_copy(whole, whole, sem).wait()

    yc = {}

    def mpack(k):
        pack(k)
        xsend(k, 1)

    def mpick(k):
        xwait(k)
        lo, hi = select(k)
        for yy in range(4):
            half = lo if yy < 2 else hi
            mom[k, yy] = half[:, 1024 * (yy % 2) : 1024 * (yy % 2) + 1024]
        yx[k, y] = mom[k, y]
        for d in (1, 3, 2):
            yc[k, d] = copy(mom.at[k, step4(y, d)], yx.at[k, y], {"y": step4(y, d)})

    def mswap(k):
        if k > 2:
            for d in (1, 3, 2):
                yc[k, d].wait_recv()
            rows = yx[k].reshape(64, 1024)
        else:
            cols = pl.ds(pl.multiple_of(y * 1024, 1024), 1024)
            rows = wall[k, z, :, :, cols].reshape(64, 1024)
        res = dot(perm64[...], rows).astype(BF)
        for u in range(4):
            for h in range(2):
                swp[k, u, h] = res[16 * u : 16 * u + 16, 512 * h : 512 * h + 512]
        msem[k] = deliver(lambda u, h: swp.at[k, u, h], fin.at[k, z * 2 + c])

    def owned(k):
        out[k] = dot(perm128[...], fin[k].reshape(128, 512)).T.astype(BF)

    def mland(k):
        landed(rsem.at[msem[k]], k, 1)
        owned(k)

    def upd(m):
        landed(gsum.at[m], 9 + m, 1)
        owned(9 + m)

    part_in[:, :, 240:, :] = jnp.zeros((3, 3, 16, 256), BF)
    pack_w(1)
    mpack(4)
    mpack(6)
    mpack(5)
    ag1(0)
    ag1(1)
    ag2(1, 0, 2)
    ag2(1, 1, 1)
    ag2(1, 0, 3)
    ag2(0, 1, 1)
    ag2(1, 1, 3)
    mpack(3)
    ag2(1, 0, 1)
    ag2(1, 1, 2)
    ag2(0, 1, 2)
    ag2(0, 1, 3)
    pack_w(2)
    ag2(0, 0, 2)
    ag2(0, 0, 3)
    ag2(0, 0, 1)
    fw(1, 0, 3)
    fw(1, 1, 0)
    fw(1, 1, 1)
    fw(1, 0, 2)
    mpack(7)
    fw(1, 1, 3)
    fw(1, 0, 1)
    fw(1, 1, 2)
    fw(1, 0, 0)
    fw(0, 1, 0)
    fw(0, 1, 3)
    fw(0, 0, 3)
    fw(0, 1, 1)
    fw(0, 0, 0)
    fw(0, 1, 2)
    fw(0, 0, 2)
    fw(0, 0, 1)
    ag1(2)
    mpack(8)
    fwd(1)
    mpick(5)
    ag2(2, 0, 1)
    mpick(8)
    fwd(0)
    ag2(2, 1, 2)
    ag2(2, 1, 1)
    ag2(2, 1, 3)
    ag2(2, 0, 2)
    ag2(2, 0, 3)
    mswap(0)
    mpick(6)
    fw(2, 0, 2)
    fw(2, 1, 1)
    fw(2, 0, 1)
    fw(2, 0, 0)
    fw(2, 1, 2)
    fw(2, 1, 0)
    mswap(5)
    fw(2, 0, 3)
    fw(2, 1, 3)
    hid()
    fwd(2)
    mswap(1)
    mswap(8)
    mland(5)
    bwd(2)
    mswap(2)
    dg(1)
    dg(0)
    mpick(7)
    mswap(6)
    rs2(2, 0)
    mpick(4)
    mpick(3)
    mland(1)
    rs2(2, 1)
    mswap(4)
    mswap(7)
    bwd(1)
    rs3(2, 0)
    rs3(2, 1)
    bwd(0)
    rs2(1, 1)
    rs2(1, 0)
    rs2(0, 1)
    rs2(0, 0)
    rs3(1, 0)
    rs5(2, 0)
    mland(2)
    rs3(1, 1)
    rs3(0, 1)
    rs3(0, 0)
    mland(4)
    rs5(2, 1)
    mswap(3)
    rs5(1, 1)
    rs5(1, 0)
    mland(0)
    mland(8)
    mland(6)
    mland(7)
    rs5(0, 1)
    rs5(0, 0)
    upd(2)
    mland(3)
    upd(1)
    upd(0)
    for d in started:
        d.wait_send()
    for same, d in late:

        @pl.when(jnp.logical_not(same))
        def _():
            d.wait_send()


def on_device(old_weights, old_first, old_second, old_blocks, owner_map, inputs, cotangent):
    any_ = pl.BlockSpec(memory_space=pl.ANY)
    smem = pl.BlockSpec(memory_space=pltpu.SMEM)
    vmem = pl.BlockSpec(memory_space=pltpu.VMEM)
    V = pltpu.VMEM
    states = pl.pallas_call(
        kernel,
        out_shape=jax.ShapeDtypeStruct((12, 512, 128), BF),
        in_specs=[smem, smem, any_, any_, any_, any_, any_],
        out_specs=vmem,
        scratch_shapes=[
            V((9, 8, 16384), F32),
            V((9, 4, 16, 2048), BF),
            V((9, 4, 16, 2048), BF),
            V((9, 4, 16, 1024), BF),
            V((9, 4, 16, 1024), BF),
            V((9, 4, 2, 16, 512), BF),
            V((12, 8, 16, 512), BF),
            V((3, 4, 4, 16, 4096), BF),
            V((4, 256, 4096), BF),
            V((4, 256, 4096), BF),
            V((3, 4, 256, 256), BF),
            V((3, 3, 256, 256), BF),
            V((3, 4, 256, 256), BF),
            V((3, 2, 4, 4, 64, 512), BF),
            V((3, 2, 2, 2, 64, 512), BF),
            V((3, 2, 2, 4, 64, 512), BF),
            V((3, 2, 4, 64, 512), BF),
            V((3, 2, 3, 64, 512), BF),
            V((3, 2, 4, 16, 512), BF),
            V((16, 64), BF),
            V((16, 64), BF),
            V((256, 256), BF),
            V((64, 64), BF),
            V((128, 128), BF),
            pltpu.SemaphoreType.DMA((NS,)),
            pltpu.SemaphoreType.DMA((NS,)),
            pltpu.SemaphoreType.DMA((16,)),
            pltpu.SemaphoreType.DMA((3,)),
        ],
        compiler_params=pltpu.CompilerParams(
            collective_id=0, has_side_effects=True, vmem_limit_bytes=64 * 1024 * 1024
        ),
        name="restore_step",
    )(
        old_blocks, owner_map.T, old_weights, old_first, old_second,
        inputs.reshape(480, 4096), cotangent.reshape(480, 16384),
    )
    w, first, second, grad = (states[3 * i : 3 * i + 3].astype(F32) for i in range(4))
    first = 0.9 * first + 0.1 * grad
    second = 0.95 * second + 0.05 * grad * grad
    w = w - 8e-05 * (first / (jnp.sqrt(second) + 1e-08) + 0.1 * w)
    return tuple(jnp.transpose(o, (1, 0, 2)) for o in (w, first, second))


def solution(mesh):
    grid = Mesh(mesh.devices.reshape(4, 4, 2, 4), ("z", "y", "c", "x"))
    dp = ("z", "y", "c")
    shard = P(None, ("z", "y", "c", "x"), None)
    in_specs = (shard, shard, shard, P(), P(), P(None, dp, "x"), P(None, dp, None))
    out_specs = (P(dp, None, "x"),) * 3
    return jax.shard_map(
        on_device, mesh=grid, in_specs=in_specs, out_specs=out_specs, check_vma=False
    )
```

```python
import functools

import jax
import jax.numpy as jnp
from jax import lax
from jax.experimental import pallas as pl
from jax.experimental.pallas import tpu as pltpu
from jax.sharding import Mesh, PartitionSpec as P

BF = jnp.bfloat16
F32 = jnp.float32
MESH = pl.DeviceIdType.MESH
NS = 98


def dot_nt(a, b):
    return lax.dot_general(a, b, (((1,), (1,)), ((), ())), preferred_element_type=F32)


def dot(a, b):
    return jnp.dot(a, b, preferred_element_type=F32)


def iota(shape, dim):
    return lax.broadcasted_iota(jnp.int32, shape, dim)


def kernel(
    blocks, owners, old_w, old_f, old_s, tok_in, cot_in,
    out,
    stage, xs, xr, mom, yx, swp, fin, wall, tok, cot, part, part_in, sgr, grd, r1, r2, ysum, r4, zed,
    sel_a, sel_b, perm, perm64, perm128,
    ssem, rsem, lsem,
):
    z, y, c, x = (lax.axis_index(a) for a in ("z", "y", "c", "x"))
    step4 = lambda v, d: lax.rem(v + d + 4, 4)
    received = {}
    SENT = ("gather", "x", "part", "share", "y", "r1", "r2", "r4", "sib", "hop")

    def sem(*name):
        return rsem.at[received.setdefault(name, len(received))]

    def copy(src, dst, dev, kind, *name):
        pltpu.make_async_remote_copy(
            src_ref=src, dst_ref=dst, send_sem=ssem.at[SENT.index(kind)],
            recv_sem=sem(kind, *name), device_id=dev, device_id_type=MESH,
        ).start()

    def arrived(like, kind, *name):
        pltpu.make_async_copy(like, like, sem(kind, *name)).wait()

    def left(like, kind):
        pltpu.make_async_copy(like, like, ssem.at[SENT.index(kind)]).wait()

    barrier = pltpu.get_barrier_semaphore()

    def greet(dev):
        pl.semaphore_signal(barrier, inc=1, device_id=dev, device_id_type=MESH)

    for d in (1, 2, 3):
        greet({"x": step4(x, d)})
        greet({"y": step4(y, d)})
    for d in (1, 3):
        greet({"z": step4(z, d)})
    greet({"c": 1 - c})
    for zs in range(4):
        for cs in range(2):
            greet({"x": z, "z": zs, "c": cs})

    olds = (old_w, old_f, old_s)
    local = []

    def load(src, dst):
        d = pltpu.make_async_copy(src, dst, lsem.at[len(local)])
        d.start()
        local.append(d)
        return d

    loads = [load(olds[k // 3].at[k % 3], stage.at[k]) for k in range(9)]
    quarter = pl.ds(pl.multiple_of(x * 4096, 4096), 4096)
    tload = []
    for mb in range(2):
        rows = pl.ds(240 * mb, 240)
        tload.append(load(tok_in.at[rows], tok.at[2 * c + mb, pl.ds(0, 240)]))
        tload.append(load(cot_in.at[rows, quarter], cot.at[2 * c + mb, pl.ds(0, 240)]))
    tok[:, 240:, :] = jnp.zeros((4, 16, 4096), BF)
    cot[:, 240:, :] = jnp.zeros((4, 16, 4096), BF)

    shape = (16, 64)
    row, col = iota(shape, 0), iota(shape, 1)
    ru, ri = row // 4, row % 4
    cx, ch, cj, cs = col // 16, (col // 8) % 2, (col // 4) % 2, col % 4
    dp = z * 8 + y * 2 + c
    group = jnp.full(shape, -1, jnp.int32)
    for xx in range(4):
        held = blocks[dp * 4 + xx]
        base = 2 * (xx // 2) + (blocks[dp * 4 + xx - 1] if xx % 2 else 0)
        for j in range(2):
            group = jnp.where((cx == xx) & (cj == j), jnp.where(j < held, base + j, -1), group)
    who = jnp.full(shape, -1, jnp.int32)
    for i in range(4):
        for s in range(4):
            who = jnp.where((ri == i) & (cs == s), owners[s, dp * 4 + i], who)
    hit = (group == ri) & (who == ru)
    sel_a[...] = jnp.where(hit & (ch == 0), 1.0, 0.0).astype(BF)
    sel_b[...] = jnp.where(hit & (ch == 1), 1.0, 0.0).astype(BF)
    r, q = iota((64, 64), 0), iota((64, 64), 1)
    want = ((r // 4) % 4) * 16 + (r // 16) * 4 + r % 4
    perm64[...] = jnp.where(q == want, 1.0, 0.0).astype(BF)
    r, q = iota((256, 256), 0), iota((256, 256), 1)
    want = (r // 64) * 64 + ((r // 4) % 4) * 16 + ((r // 16) % 4) * 4 + r % 4
    perm[...] = jnp.where(q == want, 1.0, 0.0).astype(BF)
    r, q = iota((128, 128), 0), iota((128, 128), 1)
    want = (r // 32) * 32 + ((r // 4) % 2) * 16 + ((r // 8) % 4) * 4 + r % 4
    perm128[...] = jnp.where(q == want, 1.0, 0.0).astype(BF)

    def pack(k):
        loads[k].wait()
        for xx in range(4):
            lo = stage[k, :, xx * 4096 : xx * 4096 + 2048]
            hi = stage[k, :, xx * 4096 + 2048 : xx * 4096 + 4096]
            xs[k, xx] = jnp.concatenate([lo, hi], axis=0).astype(BF)
        xr[k, x] = xs[k, x]

    pack(0)
    pl.semaphore_wait(barrier, 17)

    def xsend(k, n):
        ks = pl.ds(k, n)
        for d in (1, 3, 2):
            copy(xs.at[ks, step4(x, d)], xr.at[ks, x], {"x": step4(x, d)}, "x", k)

    xsend(0, 1)
    sib = {"c": 1 - c}
    for mb in range(2):
        rows = pl.ds(240 * mb, 240)
        copy(tok_in.at[rows], tok.at[2 * c + mb, pl.ds(0, 240)], sib, "sib", 0)
    for mb in range(2):
        rows = pl.ds(240 * mb, 240)
        copy(cot_in.at[rows, quarter], cot.at[2 * c + mb, pl.ds(0, 240)], sib, "sib", 1)

    def xwait(k):
        arrived(xr.at[k, pl.ds(0, 3)], "x", k)

    def select(k):
        rows = xr[k].reshape(64, 2048)
        return dot(sel_a[...], rows).astype(BF), dot(sel_b[...], rows).astype(BF)

    def wref(m, h, first, second, lo, n):
        cols = pl.ds(2048 * h + lo, n)
        if h == 0:
            return wall.at[m, second, first, :, cols]
        return wall.at[m, first, second, :, cols]

    def ring1(h, d):
        return {"y": step4(y, d)} if h == 0 else {"z": step4(z, d)}

    def ring2(h, d):
        return {"z": step4(z, d)} if h == 0 else {"y": step4(y, d)}

    def at1(h, d):
        return step4(y if h == 0 else z, d)

    def at2(h, d):
        return step4(z if h == 0 else y, d)

    ITEM = (0, -1, 1, 2)

    def out2(m, h, j):
        piece = wref(m, h, at1(h, ITEM[j]), at2(h, 0), 0, 2048)
        for d in (1, -1):
            copy(piece, piece, ring2(h, d), "gather", m, h, j)

    def pack_w(m):
        pack(m)
        xsend(m, 1)

    def ag1(m):
        xwait(m)
        a, b = select(m)
        wall[m, z, y, :, 0:2048] = a
        wall[m, z, y, :, 2048:4096] = b
        for h in range(2):
            piece = wref(m, h, at1(h, 0), at2(h, 0), 0, 2048)
            copy(piece, piece, ring1(h, 1), "gather", m, h, "l")
            copy(piece, piece, ring1(h, -1), "gather", m, h, "r")
        for h in range(2):
            piece = wref(m, h, at1(h, 0), at2(h, 0), 0, 2048)
            copy(piece, piece, ring1(h, 2), "gather", m, h, "o")
        for h in range(2):
            out2(m, h, 0)

    def ag2(m, h, j):
        arrived(wref(m, h, 0, 0, 0, 2048), "gather", m, h, (None, "l", "r", "o")[j])
        out2(m, h, j)

    def fw(m, h, j):
        arrived(wall.at[m, 0, pl.ds(0, 2), :, pl.ds(0, 2048)], "gather", m, h, j)
        for lo, d in ((0, 1), (1024, -1)):
            piece = wref(m, h, at1(h, ITEM[j]), at2(h, -d), lo, 1024)
            copy(piece, piece, ring2(h, d), "gather", m)

    ready = set()

    def acts_of(m):
        n = 1 if m == 2 else 0
        if n not in ready:
            ready.add(n)
            for d in tload[n::2]:
                d.wait()
            arrived((tok, cot)[n].at[pl.ds(0, 2), pl.ds(0, 240)], "sib", n)
        return (tok, cot)[n]

    def fwd(m):
        acts = acts_of(m)
        arrived(wall.at[m, pl.ds(0, 2), :, :, pl.ds(0, 2048)], "gather", m)

        rows = pl.ds(0, 240)

        def body(i, carry):
            b = step4(x, i + 1)
            part[m, b] = dot_nt(acts[b], wall[m].reshape(256, 4096)).astype(BF)

            @pl.when(i < 3)
            def _():
                copy(part.at[m, b, rows], part_in.at[m, i, rows], {"x": b}, "part", m)

            return carry

        lax.fori_loop(0, 4, body, 0)

    def summed(m):
        arrived(part_in.at[m, :, pl.ds(0, 240)], "part", m)
        total = part[m, x].astype(F32)
        for d in range(3):
            total = total + part_in[m, d].astype(F32)
        return total


    def share(m, value):
        sgr[m, x] = dot_nt(perm[...], value.astype(BF)).astype(BF)
        for d in (1, 3, 2):
            copy(sgr.at[m, x], sgr.at[m, x], {"x": step4(x, d)}, "share", m)

    kept = {}

    def hid():
        gate = summed(0)
        up = summed(1)
        sig = 1.0 / (1.0 + jnp.exp(-gate))
        act = gate * sig
        kept["act"] = act
        kept["slope"] = up * (sig * (1.0 + gate * (1.0 - sig)))
        share(2, act * up)

    def dg(m):
        if "back" not in kept:
            kept["back"] = summed(2)
        share(m, kept["back"] * kept["slope" if m == 0 else "act"])


    def bwd(m):
        acts = acts_of(m)
        arrived(sgr.at[m, pl.ds(0, 3)], "share", m)

        def body(n, carry):
            cols = pl.ds(pl.multiple_of(n * 512, 512), 512)
            left = jnp.concatenate([sgr[m, b] for b in range(4)], axis=1)
            right = acts[:, :, cols].reshape(1024, 512)
            res = dot(left, right).astype(BF).reshape(4, 64, 512)
            grd[m, lax.rem(n, 2), n // 2] = res
            return carry

        lax.fori_loop(0, 8, body, 0)
        for h in range(2):
            far = at2(h, 2)
            for half in range(2):
                if h == 0:
                    src = grd.at[m, h, pl.ds(2 * half, 2), far]
                else:
                    src = grd.at[m, h, far, pl.ds(2 * half, 2)]
                copy(src, r1.at[m, h, half], ring2(h, 1 if half == 0 else -1), "r1", m, h)

    def gref(m, h, p, q):
        return (m, h, q, p) if h == 0 else (m, h, p, q)

    def rs2(m, h):
        arrived(r1.at[m, h], "r1", m, h)
        for half in range(2):
            to = 1 if half == 0 else -1
            p = at2(h, to)
            for k in range(2):
                at = gref(m, h, p, 2 * half + k)
                grd[at] = (grd[at].astype(F32) + r1[m, h, half, k].astype(F32)).astype(BF)
            src = grd.at[m, h, :, p] if h == 0 else grd.at[m, h, p]
            copy(src, r2.at[m, h, half], ring2(h, to), "r2", m, h)

    def rs3(m, h):
        arrived(r2.at[m, h], "r2", m, h)
        for q in range(4):
            own = grd[gref(m, h, at2(h, 0), q)].astype(F32)
            ysum[m, h, q] = (
                own + r2[m, h, 0, q].astype(F32) + r2[m, h, 1, q].astype(F32)
            ).astype(BF)
        for d in (2, 1, 3):
            copy(ysum.at[m, h, at1(h, d)], r4.at[m, h, d - 1], ring1(h, d), "r4", m, h)

    def deliver(src, u, h, k):
        same = (x == z) & (x == u) & (c == h)
        dst = fin.at[k, z * 2 + c]

        @pl.when(jnp.logical_not(same))
        def _():
            copy(src, dst, {"x": u, "z": x, "c": h}, "hop", k)

        @pl.when(same)
        def _():
            pltpu.make_async_copy(src, dst, sem("hop", k)).start()

    def rs5(m, h):
        arrived(r4.at[m, h], "r4", m, h)
        own = ysum[m, h, at1(h, 0)].astype(F32)
        for d in range(3):
            own = own + r4[m, h, d].astype(F32)
        zed[m, h] = own.astype(BF).reshape(4, 16, 512)
        for u in range(4):
            deliver(zed.at[m, h, u], u, h, 9 + m)

    def landed(k):
        arrived(fin.at[k], "hop", k)


    def mpack(k):
        pack(k)
        xsend(k, 1)

    def mpick(k):
        xwait(k)
        lo, hi = select(k)
        for yy in range(4):
            half = lo if yy < 2 else hi
            mom[k, yy] = half[:, 1024 * (yy % 2) : 1024 * (yy % 2) + 1024]
        yx[k, y] = mom[k, y]
        for d in (1, 3, 2):
            copy(mom.at[k, step4(y, d)], yx.at[k, y], {"y": step4(y, d)}, "y", k)

    def mswap(k):
        if k > 2:
            arrived(yx.at[k, pl.ds(0, 3)], "y", k)
            rows = yx[k].reshape(64, 1024)
        else:
            cols = pl.ds(pl.multiple_of(y * 1024, 1024), 1024)
            rows = wall[k, z, :, :, cols].reshape(64, 1024)
        res = dot(perm64[...], rows).astype(BF)
        for u in range(4):
            for h in range(2):
                swp[k, u, h] = res[16 * u : 16 * u + 16, 512 * h : 512 * h + 512]
                deliver(swp.at[k, u, h], u, h, k)

    def owned(k):
        out[k] = dot(perm128[...], fin[k].reshape(128, 512)).T.astype(BF)

    def mland(k):
        landed(k)
        owned(k)

    def upd(m):
        landed(9 + m)
        owned(9 + m)

    part_in[:, :, 240:, :] = jnp.zeros((3, 3, 16, 256), BF)
    pack_w(1)
    mpack(4)
    mpack(6)
    mpack(5)
    ag1(0)
    ag1(1)
    ag2(1, 0, 2)
    ag2(1, 1, 1)
    ag2(1, 0, 3)
    ag2(0, 1, 1)
    ag2(1, 1, 3)
    mpack(3)
    ag2(1, 0, 1)
    ag2(1, 1, 2)
    ag2(0, 1, 2)
    ag2(0, 1, 3)
    pack_w(2)
    ag2(0, 0, 2)
    ag2(0, 0, 3)
    ag2(0, 0, 1)
    fw(1, 0, 3)
    fw(1, 1, 0)
    fw(1, 1, 1)
    fw(1, 0, 2)
    mpack(7)
    fw(1, 1, 3)
    fw(1, 0, 1)
    fw(1, 1, 2)
    fw(1, 0, 0)
    fw(0, 1, 0)
    fw(0, 1, 3)
    fw(0, 0, 3)
    fw(0, 1, 1)
    fw(0, 0, 0)
    fw(0, 1, 2)
    fw(0, 0, 2)
    fw(0, 0, 1)
    ag1(2)
    mpack(8)
    fwd(1)
    mpick(5)
    ag2(2, 0, 1)
    mpick(8)
    fwd(0)
    ag2(2, 1, 2)
    ag2(2, 1, 1)
    ag2(2, 1, 3)
    ag2(2, 0, 2)
    ag2(2, 0, 3)
    mswap(0)
    mpick(6)
    fw(2, 0, 2)
    fw(2, 1, 1)
    fw(2, 0, 1)
    fw(2, 0, 0)
    fw(2, 1, 2)
    fw(2, 1, 0)
    mswap(5)
    fw(2, 0, 3)
    fw(2, 1, 3)
    hid()
    fwd(2)
    mswap(1)
    mswap(8)
    mland(5)
    bwd(2)
    mswap(2)
    dg(1)
    dg(0)
    mpick(7)
    mswap(6)
    rs2(2, 0)
    mpick(4)
    mpick(3)
    mland(1)
    rs2(2, 1)
    mswap(4)
    mswap(7)
    bwd(1)
    rs3(2, 0)
    rs3(2, 1)
    bwd(0)
    rs2(1, 1)
    rs2(1, 0)
    rs2(0, 1)
    rs2(0, 0)
    rs3(1, 0)
    rs5(2, 0)
    mland(2)
    rs3(1, 1)
    rs3(0, 1)
    rs3(0, 0)
    mland(4)
    rs5(2, 1)
    mswap(3)
    rs5(1, 1)
    rs5(1, 0)
    mland(0)
    mland(8)
    mland(6)
    mland(7)
    rs5(0, 1)
    rs5(0, 0)
    upd(2)
    mland(3)
    upd(1)
    upd(0)
    left(tok.at[pl.ds(0, 3), pl.ds(0, 240)], "gather")
    left(xs.at[:, pl.ds(0, 3)], "x")
    left(part_in.at[:, :, pl.ds(0, 240)], "part")
    left(part_in, "share")
    left(yx.at[pl.ds(0, 6), pl.ds(0, 3)], "y")
    left(r1, "r1")
    left(r2, "r2")
    left(r4, "r4")
    left(tok.at[:, pl.ds(0, 240)], "sib")

    @pl.when(x == z)
    def _():
        left(fin.at[:, pl.ds(0, 7)], "hop")

    @pl.when(x != z)
    def _():
        left(fin, "hop")

    assert len(received) == NS, len(received)


def on_device(old_weights, old_first, old_second, old_blocks, owner_map, inputs, cotangent):
    any_ = pl.BlockSpec(memory_space=pl.ANY)
    smem = pl.BlockSpec(memory_space=pltpu.SMEM)
    vmem = pl.BlockSpec(memory_space=pltpu.VMEM)
    V = pltpu.VMEM
    states = pl.pallas_call(
        kernel,
        out_shape=jax.ShapeDtypeStruct((12, 512, 128), BF),
        in_specs=[smem, smem, any_, any_, any_, any_, any_],
        out_specs=vmem,
        scratch_shapes=[
            V((9, 8, 16384), F32),
            V((9, 4, 16, 2048), BF),
            V((9, 4, 16, 2048), BF),
            V((9, 4, 16, 1024), BF),
            V((9, 4, 16, 1024), BF),
            V((9, 4, 2, 16, 512), BF),
            V((12, 8, 16, 512), BF),
            V((3, 4, 4, 16, 4096), BF),
            V((4, 256, 4096), BF),
            V((4, 256, 4096), BF),
            V((3, 4, 256, 256), BF),
            V((3, 3, 256, 256), BF),
            V((3, 4, 256, 256), BF),
            V((3, 2, 4, 4, 64, 512), BF),
            V((3, 2, 2, 2, 64, 512), BF),
            V((3, 2, 2, 4, 64, 512), BF),
            V((3, 2, 4, 64, 512), BF),
            V((3, 2, 3, 64, 512), BF),
            V((3, 2, 4, 16, 512), BF),
            V((16, 64), BF),
            V((16, 64), BF),
            V((256, 256), BF),
            V((64, 64), BF),
            V((128, 128), BF),
            pltpu.SemaphoreType.DMA((10,)),
            pltpu.SemaphoreType.DMA((NS,)),
            pltpu.SemaphoreType.DMA((13,)),
        ],
        compiler_params=pltpu.CompilerParams(
            collective_id=0, has_side_effects=True, vmem_limit_bytes=64 * 1024 * 1024
        ),
        name="restore_step",
    )(
        old_blocks, owner_map.T, old_weights, old_first, old_second,
        inputs.reshape(480, 4096), cotangent.reshape(480, 16384),
    )
    w, first, second, grad = (states[3 * i : 3 * i + 3].astype(F32) for i in range(4))
    first = 0.9 * first + 0.1 * grad
    second = 0.95 * second + 0.05 * grad * grad
    w = w - 8e-05 * (first / (jnp.sqrt(second) + 1e-08) + 0.1 * w)
    return tuple(jnp.transpose(o, (1, 0, 2)) for o in (w, first, second))


def solution(mesh):
    grid = Mesh(mesh.devices.reshape(4, 4, 2, 4), ("z", "y", "c", "x"))
    dp = ("z", "y", "c")
    shard = P(None, ("z", "y", "c", "x"), None)
    in_specs = (shard, shard, shard, P(), P(), P(None, dp, "x"), P(None, dp, None))
    out_specs = (P(dp, None, "x"),) * 3
    return jax.shard_map(
        on_device, mesh=grid, in_specs=in_specs, out_specs=out_specs, check_vma=False
    )
```

```python
import functools

import jax
import jax.numpy as jnp
from jax import lax
from jax.experimental import pallas as pl
from jax.experimental.pallas import tpu as pltpu
from jax.sharding import Mesh, PartitionSpec as P

BF = jnp.bfloat16
F32 = jnp.float32
MESH = pl.DeviceIdType.MESH
NS = 98


def dot_nt(a, b):
    return lax.dot_general(a, b, (((1,), (1,)), ((), ())), preferred_element_type=F32)


def dot(a, b):
    return jnp.dot(a, b, preferred_element_type=F32)


def iota(shape, dim):
    return lax.broadcasted_iota(jnp.int32, shape, dim)


def kernel(
    blocks_in, owners_in, old_w, old_f, old_s, tok_in, cot_in,
    out,
    stage, xs, xr, mom, yx, swp, fin, wall, tok, cot, part, part_in, sgr, grd, r1, r2, ysum, r4, zed,
    sel_a, sel_b, perm, perm64, perm128, blocks, owners, moved,
    ssem, rsem, lsem, osem,
):
    z, y, c, x = (lax.axis_index(a) for a in ("z", "y", "c", "x"))
    step4 = lambda v, d: lax.rem(v + d + 4, 4)
    received = {}
    SENT = ("gather", "x", "part", "share", "y", "r1", "r2", "r4", "sib", "hop")

    def sem(*name):
        return rsem.at[received.setdefault(name, len(received))]

    def copy(src, dst, dev, kind, *name):
        pltpu.make_async_remote_copy(
            src_ref=src, dst_ref=dst, send_sem=ssem.at[SENT.index(kind)],
            recv_sem=sem(kind, *name), device_id=dev, device_id_type=MESH,
        ).start()

    def arrived(like, kind, *name):
        pltpu.make_async_copy(like, like, sem(kind, *name)).wait()

    def left(like, kind):
        pltpu.make_async_copy(like, like, ssem.at[SENT.index(kind)]).wait()

    barrier = pltpu.get_barrier_semaphore()

    def greet(dev):
        pl.semaphore_signal(barrier, inc=1, device_id=dev, device_id_type=MESH)

    for d in (1, 2, 3):
        greet({"x": step4(x, d)})
        greet({"y": step4(y, d)})
    for d in (1, 3):
        greet({"z": step4(z, d)})
    greet({"c": 1 - c})
    for zs in range(4):
        for cs in range(2):
            greet({"x": z, "z": zs, "c": cs})

    olds = (old_w, old_f, old_s)
    local = []

    def load(src, dst):
        d = pltpu.make_async_copy(src, dst, lsem.at[len(local)])
        d.start()
        local.append(d)
        return d

    few = [load(blocks_in, blocks), load(owners_in, owners)]
    loads = [load(olds[k // 3].at[k % 3], stage.at[k]) for k in range(9)]
    quarter = pl.ds(pl.multiple_of(x * 4096, 4096), 4096)
    tload = []
    for mb in range(2):
        rows = pl.ds(240 * mb, 240)
        tload.append(load(tok_in.at[rows], tok.at[2 * c + mb, pl.ds(0, 240)]))
        tload.append(load(cot_in.at[rows, quarter], cot.at[2 * c + mb, pl.ds(0, 240)]))
    tok[:, 240:, :] = jnp.zeros((4, 16, 4096), BF)
    cot[:, 240:, :] = jnp.zeros((4, 16, 4096), BF)

    for d in few:
        d.wait()

    shape = (16, 64)
    row, col = iota(shape, 0), iota(shape, 1)
    ru, ri = row // 4, row % 4
    cx, ch, cj, cs = col // 16, (col // 8) % 2, (col // 4) % 2, col % 4
    dp = z * 8 + y * 2 + c
    group = jnp.full(shape, -1, jnp.int32)
    for xx in range(4):
        held = blocks[dp * 4 + xx]
        base = 2 * (xx // 2) + (blocks[dp * 4 + xx - 1] if xx % 2 else 0)
        for j in range(2):
            group = jnp.where((cx == xx) & (cj == j), jnp.where(j < held, base + j, -1), group)
    who = jnp.full(shape, -1, jnp.int32)
    for i in range(4):
        for s in range(4):
            who = jnp.where((ri == i) & (cs == s), owners[s, dp * 4 + i], who)
    hit = (group == ri) & (who == ru)
    sel_a[...] = jnp.where(hit & (ch == 0), 1.0, 0.0).astype(BF)
    sel_b[...] = jnp.where(hit & (ch == 1), 1.0, 0.0).astype(BF)
    r, q = iota((64, 64), 0), iota((64, 64), 1)
    want = ((r // 4) % 4) * 16 + (r // 16) * 4 + r % 4
    perm64[...] = jnp.where(q == want, 1.0, 0.0).astype(BF)
    r, q = iota((256, 256), 0), iota((256, 256), 1)
    want = (r // 64) * 64 + ((r // 4) % 4) * 16 + ((r // 16) % 4) * 4 + r % 4
    perm[...] = jnp.where(q == want, 1.0, 0.0).astype(BF)
    r, q = iota((128, 128), 0), iota((128, 128), 1)
    want = (r // 32) * 32 + ((r // 4) % 2) * 16 + ((r // 8) % 4) * 4 + r % 4
    perm128[...] = jnp.where(q == want, 1.0, 0.0).astype(BF)

    def pack(k):
        loads[k].wait()
        for xx in range(4):
            lo = stage[k, :, xx * 4096 : xx * 4096 + 2048]
            hi = stage[k, :, xx * 4096 + 2048 : xx * 4096 + 4096]
            xs[k, xx] = jnp.concatenate([lo, hi], axis=0).astype(BF)
        xr[k, x] = xs[k, x]

    pack(0)
    pl.semaphore_wait(barrier, 17)

    def xsend(k, n):
        ks = pl.ds(k, n)
        for d in (1, 3, 2):
            copy(xs.at[ks, step4(x, d)], xr.at[ks, x], {"x": step4(x, d)}, "x", k)

    xsend(0, 1)
    sib = {"c": 1 - c}
    for mb in range(2):
        rows = pl.ds(240 * mb, 240)
        copy(tok_in.at[rows], tok.at[2 * c + mb, pl.ds(0, 240)], sib, "sib", 0)
    for mb in range(2):
        rows = pl.ds(240 * mb, 240)
        copy(cot_in.at[rows, quarter], cot.at[2 * c + mb, pl.ds(0, 240)], sib, "sib", 1)

    def xwait(k):
        arrived(xr.at[k, pl.ds(0, 3)], "x", k)

    def select(k):
        rows = xr[k].reshape(64, 2048)
        return dot(sel_a[...], rows).astype(BF), dot(sel_b[...], rows).astype(BF)

    def wref(m, h, first, second, lo, n):
        cols = pl.ds(2048 * h + lo, n)
        if h == 0:
            return wall.at[m, second, first, :, cols]
        return wall.at[m, first, second, :, cols]

    def ring1(h, d):
        return {"y": step4(y, d)} if h == 0 else {"z": step4(z, d)}

    def ring2(h, d):
        return {"z": step4(z, d)} if h == 0 else {"y": step4(y, d)}

    def at1(h, d):
        return step4(y if h == 0 else z, d)

    def at2(h, d):
        return step4(z if h == 0 else y, d)

    ITEM = (0, -1, 1, 2)

    def out2(m, h, j):
        piece = wref(m, h, at1(h, ITEM[j]), at2(h, 0), 0, 2048)
        for d in (1, -1):
            copy(piece, piece, ring2(h, d), "gather", m, h, j)

    def pack_w(m):
        pack(m)
        xsend(m, 1)

    def ag1(m):
        xwait(m)
        a, b = select(m)
        wall[m, z, y, :, 0:2048] = a
        wall[m, z, y, :, 2048:4096] = b
        for h in range(2):
            piece = wref(m, h, at1(h, 0), at2(h, 0), 0, 2048)
            copy(piece, piece, ring1(h, 1), "gather", m, h, "l")
            copy(piece, piece, ring1(h, -1), "gather", m, h, "r")
        for h in range(2):
            piece = wref(m, h, at1(h, 0), at2(h, 0), 0, 2048)
            copy(piece, piece, ring1(h, 2), "gather", m, h, "o")
        for h in range(2):
            out2(m, h, 0)

    def ag2(m, h, j):
        arrived(wref(m, h, 0, 0, 0, 2048), "gather", m, h, (None, "l", "r", "o")[j])
        out2(m, h, j)

    def fw(m, h, j):
        arrived(wall.at[m, 0, pl.ds(0, 2), :, pl.ds(0, 2048)], "gather", m, h, j)
        for lo, d in ((0, 1), (1024, -1)):
            piece = wref(m, h, at1(h, ITEM[j]), at2(h, -d), lo, 1024)
            copy(piece, piece, ring2(h, d), "gather", m)

    ready = set()

    def acts_of(m):
        n = 1 if m == 2 else 0
        if n not in ready:
            ready.add(n)
            for d in tload[n::2]:
                d.wait()
            arrived((tok, cot)[n].at[pl.ds(0, 2), pl.ds(0, 240)], "sib", n)
        return (tok, cot)[n]

    def fwd(m):
        acts = acts_of(m)
        arrived(wall.at[m, pl.ds(0, 2), :, :, pl.ds(0, 2048)], "gather", m)

        rows = pl.ds(0, 240)

        def body(i, carry):
            b = step4(x, i + 1)
            part[m, b] = dot_nt(acts[b], wall[m].reshape(256, 4096)).astype(BF)

            @pl.when(i < 3)
            def _():
                copy(part.at[m, b, rows], part_in.at[m, i, rows], {"x": b}, "part", m)

            return carry

        lax.fori_loop(0, 4, body, 0)

    def summed(m):
        arrived(part_in.at[m, :, pl.ds(0, 240)], "part", m)
        total = part[m, x].astype(F32)
        for d in range(3):
            total = total + part_in[m, d].astype(F32)
        return total


    def share(m, value):
        sgr[m, x] = dot_nt(perm[...], value.astype(BF)).astype(BF)
        for d in (1, 3, 2):
            copy(sgr.at[m, x], sgr.at[m, x], {"x": step4(x, d)}, "share", m)

    kept = {}

    def hid():
        gate = summed(0)
        up = summed(1)
        sig = 1.0 / (1.0 + jnp.exp(-gate))
        act = gate * sig
        kept["act"] = act
        kept["slope"] = up * (sig * (1.0 + gate * (1.0 - sig)))
        share(2, act * up)

    def dg(m):
        if "back" not in kept:
            kept["back"] = summed(2)
        share(m, kept["back"] * kept["slope" if m == 0 else "act"])


    def bwd(m):
        acts = acts_of(m)
        arrived(sgr.at[m, pl.ds(0, 3)], "share", m)

        def body(n, carry):
            cols = pl.ds(pl.multiple_of(n * 512, 512), 512)
            left = jnp.concatenate([sgr[m, b] for b in range(4)], axis=1)
            right = acts[:, :, cols].reshape(1024, 512)
            res = dot(left, right).astype(BF).reshape(4, 64, 512)
            grd[m, lax.rem(n, 2), n // 2] = res
            return carry

        lax.fori_loop(0, 8, body, 0)
        for h in range(2):
            far = at2(h, 2)
            for half in range(2):
                if h == 0:
                    src = grd.at[m, h, pl.ds(2 * half, 2), far]
                else:
                    src = grd.at[m, h, far, pl.ds(2 * half, 2)]
                copy(src, r1.at[m, h, half], ring2(h, 1 if half == 0 else -1), "r1", m, h)

    def gref(m, h, p, q):
        return (m, h, q, p) if h == 0 else (m, h, p, q)

    def rs2(m, h):
        arrived(r1.at[m, h], "r1", m, h)
        for half in range(2):
            to = 1 if half == 0 else -1
            p = at2(h, to)
            for k in range(2):
                at = gref(m, h, p, 2 * half + k)
                grd[at] = (grd[at].astype(F32) + r1[m, h, half, k].astype(F32)).astype(BF)
            src = grd.at[m, h, :, p] if h == 0 else grd.at[m, h, p]
            copy(src, r2.at[m, h, half], ring2(h, to), "r2", m, h)

    def rs3(m, h):
        arrived(r2.at[m, h], "r2", m, h)
        for q in range(4):
            own = grd[gref(m, h, at2(h, 0), q)].astype(F32)
            ysum[m, h, q] = (
                own + r2[m, h, 0, q].astype(F32) + r2[m, h, 1, q].astype(F32)
            ).astype(BF)
        for d in (2, 1, 3):
            copy(ysum.at[m, h, at1(h, d)], r4.at[m, h, d - 1], ring1(h, d), "r4", m, h)

    def deliver(src, u, h, k):
        same = (x == z) & (x == u) & (c == h)
        dst = fin.at[k, z * 2 + c]

        @pl.when(jnp.logical_not(same))
        def _():
            copy(src, dst, {"x": u, "z": x, "c": h}, "hop", k)

        @pl.when(same)
        def _():
            pltpu.make_async_copy(src, dst, sem("hop", k)).start()

    def rs5(m, h):
        arrived(r4.at[m, h], "r4", m, h)
        own = ysum[m, h, at1(h, 0)].astype(F32)
        for d in range(3):
            own = own + r4[m, h, d].astype(F32)
        zed[m, h] = own.astype(BF).reshape(4, 16, 512)
        for u in range(4):
            deliver(zed.at[m, h, u], u, h, 9 + m)

    def landed(k):
        arrived(fin.at[k], "hop", k)


    def mpack(k):
        pack(k)
        xsend(k, 1)

    def mpick(k):
        xwait(k)
        lo, hi = select(k)
        for yy in range(4):
            half = lo if yy < 2 else hi
            mom[k, yy] = half[:, 1024 * (yy % 2) : 1024 * (yy % 2) + 1024]
        yx[k, y] = mom[k, y]
        for d in (1, 3, 2):
            copy(mom.at[k, step4(y, d)], yx.at[k, y], {"y": step4(y, d)}, "y", k)

    def mswap(k):
        if k > 2:
            arrived(yx.at[k, pl.ds(0, 3)], "y", k)
            rows = yx[k].reshape(64, 1024)
        else:
            cols = pl.ds(pl.multiple_of(y * 1024, 1024), 1024)
            rows = wall[k, z, :, :, cols].reshape(64, 1024)
        res = dot(perm64[...], rows).astype(BF)
        for u in range(4):
            for h in range(2):
                swp[k, u, h] = res[16 * u : 16 * u + 16, 512 * h : 512 * h + 512]
                deliver(swp.at[k, u, h], u, h, k)

    def owned(k):
        moved[k] = dot(perm128[...], fin[k].reshape(128, 512)).T.astype(BF)
        pltpu.make_async_copy(moved.at[k], out.at[k], osem).start()

    def mland(k):
        landed(k)
        owned(k)

    def upd(m):
        landed(9 + m)
        owned(9 + m)

    part_in[:, :, 240:, :] = jnp.zeros((3, 3, 16, 256), BF)
    pack_w(1)
    ag1(0)
    pack_w(2)
    mpack(6)
    ag1(1)
    ag2(0, 0, 3)
    mpack(3)
    ag2(0, 1, 3)
    ag2(1, 0, 3)
    ag2(1, 1, 1)
    ag2(1, 1, 2)
    ag2(1, 0, 2)
    ag2(1, 1, 3)
    ag2(1, 0, 1)
    mpack(4)
    fw(1, 0, 0)
    ag2(0, 0, 1)
    mpack(5)
    ag2(0, 1, 1)
    fw(1, 1, 0)
    fw(1, 1, 1)
    ag2(0, 1, 2)
    ag2(0, 0, 2)
    fw(1, 0, 1)
    fw(1, 1, 3)
    fw(1, 1, 2)
    fw(1, 0, 3)
    mpack(7)
    fw(1, 0, 2)
    mpack(8)
    fw(0, 0, 0)
    fw(0, 1, 3)
    fw(0, 1, 0)
    fw(0, 1, 1)
    fw(0, 0, 3)
    fw(0, 0, 2)
    fw(0, 1, 2)
    fw(0, 0, 1)
    ag1(2)
    mpick(5)
    fwd(1)
    fwd(0)
    ag2(2, 0, 2)
    ag2(2, 1, 1)
    ag2(2, 1, 3)
    ag2(2, 1, 2)
    mpick(6)
    ag2(2, 0, 3)
    ag2(2, 0, 1)
    mpick(4)
    fw(2, 0, 0)
    fw(2, 1, 1)
    mswap(1)
    mpick(3)
    fw(2, 1, 3)
    fw(2, 1, 0)
    fw(2, 0, 2)
    fw(2, 0, 1)
    mswap(5)
    fw(2, 1, 2)
    hid()
    fw(2, 0, 3)
    fwd(2)
    mpick(8)
    mswap(0)
    mswap(6)
    bwd(2)
    mswap(8)
    dg(1)
    mpick(7)
    dg(0)
    mswap(4)
    mswap(2)
    rs2(2, 0)
    rs2(2, 1)
    mswap(7)
    bwd(1)
    rs3(2, 1)
    mland(1)
    rs3(2, 0)
    bwd(0)
    rs2(1, 0)
    rs2(1, 1)
    mland(0)
    rs2(0, 0)
    mland(4)
    rs2(0, 1)
    mland(7)
    rs5(2, 1)
    rs3(1, 0)
    rs3(1, 1)
    rs3(0, 1)
    rs3(0, 0)
    mland(6)
    mland(2)
    rs5(2, 0)
    mswap(3)
    rs5(1, 0)
    mland(5)
    mland(8)
    rs5(1, 1)
    rs5(0, 1)
    rs5(0, 0)
    upd(2)
    mland(3)
    upd(1)
    upd(0)
    pltpu.make_async_copy(moved, out, osem).wait()
    left(tok.at[pl.ds(0, 3), pl.ds(0, 240)], "gather")
    left(xs.at[:, pl.ds(0, 3)], "x")
    left(part_in.at[:, :, pl.ds(0, 240)], "part")
    left(part_in, "share")
    left(yx.at[pl.ds(0, 6), pl.ds(0, 3)], "y")
    left(r1, "r1")
    left(r2, "r2")
    left(r4, "r4")
    left(tok.at[:, pl.ds(0, 240)], "sib")

    @pl.when(x == z)
    def _():
        left(fin.at[:, pl.ds(0, 7)], "hop")

    @pl.when(x != z)
    def _():
        left(fin, "hop")

    assert len(received) == NS, len(received)


def on_device(old_weights, old_first, old_second, old_blocks, owner_map, inputs, cotangent):
    any_ = pl.BlockSpec(memory_space=pl.ANY)
    V = pltpu.VMEM
    states = pl.pallas_call(
        kernel,
        out_shape=jax.ShapeDtypeStruct((12, 512, 128), BF),
        in_specs=[any_, any_, any_, any_, any_, any_, any_],
        out_specs=any_,
        scratch_shapes=[
            V((9, 8, 16384), F32),
            V((9, 4, 16, 2048), BF),
            V((9, 4, 16, 2048), BF),
            V((9, 4, 16, 1024), BF),
            V((9, 4, 16, 1024), BF),
            V((9, 4, 2, 16, 512), BF),
            V((12, 8, 16, 512), BF),
            V((3, 4, 4, 16, 4096), BF),
            V((4, 256, 4096), BF),
            V((4, 256, 4096), BF),
            V((3, 4, 256, 256), BF),
            V((3, 3, 256, 256), BF),
            V((3, 4, 256, 256), BF),
            V((3, 2, 4, 4, 64, 512), BF),
            V((3, 2, 2, 2, 64, 512), BF),
            V((3, 2, 2, 4, 64, 512), BF),
            V((3, 2, 4, 64, 512), BF),
            V((3, 2, 3, 64, 512), BF),
            V((3, 2, 4, 16, 512), BF),
            V((16, 64), BF),
            V((16, 64), BF),
            V((256, 256), BF),
            V((64, 64), BF),
            V((128, 128), BF),
            pltpu.SMEM((128,), jnp.int32),
            pltpu.SMEM((4, 128), jnp.int32),
            V((12, 512, 128), BF),
            pltpu.SemaphoreType.DMA((10,)),
            pltpu.SemaphoreType.DMA((NS,)),
            pltpu.SemaphoreType.DMA((15,)),
            pltpu.SemaphoreType.DMA,
        ],
        compiler_params=pltpu.CompilerParams(
            collective_id=0, has_side_effects=True, vmem_limit_bytes=64 * 1024 * 1024
        ),
        name="restore_step",
    )(
        old_blocks, owner_map.T, old_weights, old_first, old_second,
        inputs.reshape(480, 4096), cotangent.reshape(480, 16384),
    )
    w, first, second, grad = (states[3 * i : 3 * i + 3].astype(F32) for i in range(4))
    first = 0.9 * first + 0.1 * grad
    second = 0.95 * second + 0.05 * grad * grad
    w = w - 8e-05 * (first / (jnp.sqrt(second) + 1e-08) + 0.1 * w)
    return tuple(jnp.transpose(o, (1, 0, 2)) for o in (w, first, second))


def solution(mesh):
    grid = Mesh(mesh.devices.reshape(4, 4, 2, 4), ("z", "y", "c", "x"))
    dp = ("z", "y", "c")
    shard = P(None, ("z", "y", "c", "x"), None)
    in_specs = (shard, shard, shard, P(), P(), P(None, dp, "x"), P(None, dp, None))
    out_specs = (P(dp, None, "x"),) * 3
    return jax.shard_map(
        on_device, mesh=grid, in_specs=in_specs, out_specs=out_specs, check_vma=False
    )
```

```python
import functools

import jax
import jax.numpy as jnp
from jax import lax
from jax.experimental import pallas as pl
from jax.experimental.pallas import tpu as pltpu
from jax.sharding import Mesh, PartitionSpec as P

BF = jnp.bfloat16
F32 = jnp.float32
MESH = pl.DeviceIdType.MESH
NS = 98


def dot_nt(a, b):
    return lax.dot_general(a, b, (((1,), (1,)), ((), ())), preferred_element_type=F32)


def dot(a, b):
    return jnp.dot(a, b, preferred_element_type=F32)


def iota(shape, dim):
    return lax.broadcasted_iota(jnp.int32, shape, dim)


def kernel(
    blocks_in, owners_in, old_w, old_f, old_s, tok_in, cot_in,
    out,
    stage, xs, xr, mom, yx, swp, fin, wall, tok, cot, part, part_in, sgr, grd, r1, r2, ysum, r4, zed,
    sel_a, sel_b, perm, perm64, perm128, blocks, owners, moved,
    ssem, rsem, lsem, osem,
):
    z, y, c, x = (lax.axis_index(a) for a in ("z", "y", "c", "x"))
    step4 = lambda v, d: lax.rem(v + d + 4, 4)
    received = {}
    SENT = ("gather", "x", "part", "share", "y", "r1", "r2", "r4", "sib", "hop")

    def sem(*name):
        return rsem.at[received.setdefault(name, len(received))]

    def copy(src, dst, dev, kind, *name):
        pltpu.make_async_remote_copy(
            src_ref=src, dst_ref=dst, send_sem=ssem.at[SENT.index(kind)],
            recv_sem=sem(kind, *name), device_id=dev, device_id_type=MESH,
        ).start()

    def arrived(like, kind, *name):
        pltpu.make_async_copy(like, like, sem(kind, *name)).wait()

    def left(like, kind):
        pltpu.make_async_copy(like, like, ssem.at[SENT.index(kind)]).wait()

    barrier = pltpu.get_barrier_semaphore()

    def greet(dev):
        pl.semaphore_signal(barrier, inc=1, device_id=dev, device_id_type=MESH)

    for d in (1, 2, 3):
        greet({"x": step4(x, d)})
        greet({"y": step4(y, d)})
    for d in (1, 3):
        greet({"z": step4(z, d)})
    greet({"c": 1 - c})
    for zs in range(4):
        for cs in range(2):
            greet({"x": z, "z": zs, "c": cs})

    olds = (old_w, old_f, old_s)
    local = []

    def load(src, dst):
        d = pltpu.make_async_copy(src, dst, lsem.at[len(local)])
        d.start()
        local.append(d)
        return d

    few = [load(blocks_in, blocks), load(owners_in, owners)]
    loads = [load(olds[k // 3].at[k % 3], stage.at[k]) for k in range(9)]
    quarter = pl.ds(pl.multiple_of(x * 4096, 4096), 4096)
    tload = []
    for mb in range(2):
        rows = pl.ds(240 * mb, 240)
        tload.append(load(tok_in.at[rows], tok.at[2 * c + mb, pl.ds(0, 240)]))
        tload.append(load(cot_in.at[rows, quarter], cot.at[2 * c + mb, pl.ds(0, 240)]))
    tok[:, 240:, :] = jnp.zeros((4, 16, 4096), BF)
    cot[:, 240:, :] = jnp.zeros((4, 16, 4096), BF)

    for d in few:
        d.wait()

    shape = (16, 64)
    row, col = iota(shape, 0), iota(shape, 1)
    ru, ri = row // 4, row % 4
    cx, ch, cj, cs = col // 16, (col // 8) % 2, (col // 4) % 2, col % 4
    dp = z * 8 + y * 2 + c
    group = jnp.full(shape, -1, jnp.int32)
    for xx in range(4):
        held = blocks[dp * 4 + xx]
        base = 2 * (xx // 2) + (blocks[dp * 4 + xx - 1] if xx % 2 else 0)
        for j in range(2):
            group = jnp.where((cx == xx) & (cj == j), jnp.where(j < held, base + j, -1), group)
    who = jnp.full(shape, -1, jnp.int32)
    for i in range(4):
        for s in range(4):
            who = jnp.where((ri == i) & (cs == s), owners[s, dp * 4 + i], who)
    hit = (group == ri) & (who == ru)
    sel_a[...] = jnp.where(hit & (ch == 0), 1.0, 0.0).astype(BF)
    sel_b[...] = jnp.where(hit & (ch == 1), 1.0, 0.0).astype(BF)
    r, q = iota((64, 64), 0), iota((64, 64), 1)
    want = ((r // 4) % 4) * 16 + (r // 16) * 4 + r % 4
    perm64[...] = jnp.where(q == want, 1.0, 0.0).astype(BF)
    r, q = iota((256, 256), 0), iota((256, 256), 1)
    want = (r // 64) * 64 + ((r // 4) % 4) * 16 + ((r // 16) % 4) * 4 + r % 4
    perm[...] = jnp.where(q == want, 1.0, 0.0).astype(BF)
    r, q = iota((128, 128), 0), iota((128, 128), 1)
    want = (r // 32) * 32 + ((r // 4) % 2) * 16 + ((r // 8) % 4) * 4 + r % 4
    perm128[...] = jnp.where(q == want, 1.0, 0.0).astype(BF)

    def pack(k):
        loads[k].wait()
        for xx in range(4):
            lo = stage[k, :, xx * 4096 : xx * 4096 + 2048]
            hi = stage[k, :, xx * 4096 + 2048 : xx * 4096 + 4096]
            xs[k, xx] = jnp.concatenate([lo, hi], axis=0).astype(BF)
        xr[k, x] = xs[k, x]

    pack(0)
    pl.semaphore_wait(barrier, 17)

    def xsend(k, n):
        ks = pl.ds(k, n)
        for d in (1, 3, 2):
            copy(xs.at[ks, step4(x, d)], xr.at[ks, x], {"x": step4(x, d)}, "x", k)

    xsend(0, 1)
    sib = {"c": 1 - c}
    for mb in range(2):
        rows = pl.ds(240 * mb, 240)
        copy(tok_in.at[rows], tok.at[2 * c + mb, pl.ds(0, 240)], sib, "sib", 0)
    for mb in range(2):
        rows = pl.ds(240 * mb, 240)
        copy(cot_in.at[rows, quarter], cot.at[2 * c + mb, pl.ds(0, 240)], sib, "sib", 1)

    def xwait(k):
        arrived(xr.at[k, pl.ds(0, 3)], "x", k)

    def select(k):
        rows = xr[k].reshape(64, 2048)
        return dot(sel_a[...], rows).astype(BF), dot(sel_b[...], rows).astype(BF)

    def wref(m, h, first, second, lo, n):
        cols = pl.ds(2048 * h + lo, n)
        if h == 0:
            return wall.at[m, second, first, :, cols]
        return wall.at[m, first, second, :, cols]

    def ring1(h, d):
        return {"y": step4(y, d)} if h == 0 else {"z": step4(z, d)}

    def ring2(h, d):
        return {"z": step4(z, d)} if h == 0 else {"y": step4(y, d)}

    def at1(h, d):
        return step4(y if h == 0 else z, d)

    def at2(h, d):
        return step4(z if h == 0 else y, d)

    ITEM = (0, -1, 1, 2)

    def out2(m, h, j):
        piece = wref(m, h, at1(h, ITEM[j]), at2(h, 0), 0, 2048)
        for d in (1, -1):
            copy(piece, piece, ring2(h, d), "gather", m, h, j)

    def pack_w(m):
        pack(m)
        xsend(m, 1)

    def ag1(m):
        xwait(m)
        a, b = select(m)
        wall[m, z, y, :, 0:2048] = a
        wall[m, z, y, :, 2048:4096] = b
        for h in range(2):
            piece = wref(m, h, at1(h, 0), at2(h, 0), 0, 2048)
            copy(piece, piece, ring1(h, 1), "gather", m, h, "l")
            copy(piece, piece, ring1(h, -1), "gather", m, h, "r")
        for h in range(2):
            piece = wref(m, h, at1(h, 0), at2(h, 0), 0, 2048)
            copy(piece, piece, ring1(h, 2), "gather", m, h, "o")
        for h in range(2):
            out2(m, h, 0)

    def ag2(m, h, j):
        arrived(wref(m, h, 0, 0, 0, 2048), "gather", m, h, (None, "l", "r", "o")[j])
        out2(m, h, j)

    def fw(m, h, j):
        arrived(wall.at[m, 0, pl.ds(0, 2), :, pl.ds(0, 2048)], "gather", m, h, j)
        for lo, d in ((0, 1), (1024, -1)):
            piece = wref(m, h, at1(h, ITEM[j]), at2(h, -d), lo, 1024)
            copy(piece, piece, ring2(h, d), "gather", m)

    ready = set()

    def acts_of(m):
        n = 1 if m == 2 else 0
        if n not in ready:
            ready.add(n)
            for d in tload[n::2]:
                d.wait()
            arrived((tok, cot)[n].at[pl.ds(0, 2), pl.ds(0, 240)], "sib", n)
        return (tok, cot)[n]

    def fwd(m):
        acts = acts_of(m)
        arrived(wall.at[m, pl.ds(0, 2), :, :, pl.ds(0, 2048)], "gather", m)

        rows = pl.ds(0, 240)

        def body(i, carry):
            b = step4(x, i + 1)
            part[m, b] = dot_nt(acts[b], wall[m].reshape(256, 4096)).astype(BF)

            @pl.when(i < 3)
            def _():
                copy(part.at[m, b, rows], part_in.at[m, i, rows], {"x": b}, "part", m)

            return carry

        lax.fori_loop(0, 4, body, 0)

    def summed(m):
        arrived(part_in.at[m, :, pl.ds(0, 240)], "part", m)
        total = part[m, x].astype(F32)
        for d in range(3):
            total = total + part_in[m, d].astype(F32)
        return total


    def share(m, value):
        sgr[m, x] = dot_nt(perm[...], value.astype(BF)).astype(BF)
        for d in (1, 3, 2):
            copy(sgr.at[m, x], sgr.at[m, x], {"x": step4(x, d)}, "share", m)

    kept = {}

    def hid():
        gate = summed(0)
        up = summed(1)
        sig = 1.0 / (1.0 + jnp.exp(-gate))
        act = gate * sig
        kept["act"] = act
        kept["slope"] = up * (sig * (1.0 + gate * (1.0 - sig)))
        share(2, act * up)

    def dg(m):
        if "back" not in kept:
            kept["back"] = summed(2)
        share(m, kept["back"] * kept["slope" if m == 0 else "act"])


    def bwd(m):
        acts = acts_of(m)
        arrived(sgr.at[m, pl.ds(0, 3)], "share", m)

        def block(yy, h):
            cols = pl.ds(pl.multiple_of(yy * 1024 + h * 512, 512), 512)
            left = jnp.concatenate([sgr[m, b] for b in range(4)], axis=1)
            right = acts[:, :, cols].reshape(1024, 512)
            grd[m, h, yy] = dot(left, right).astype(BF).reshape(4, 64, 512)

        def blocks(first, n, h):
            def body(i, carry):
                block(step4(first, i), h)
                return carry

            lax.fori_loop(0, n, body, 0)

        def send(h, half):
            far = at2(h, 2)
            pair = pl.ds(2 * half, 2)
            src = grd.at[m, h, pair, far] if h == 0 else grd.at[m, h, far, pair]
            copy(src, r1.at[m, h, half], ring2(h, 1 if half == 0 else -1), "r1", m, h)

        block(step4(y, 2), 1)
        send(1, 0)
        send(1, 1)
        blocks(0, 4, 0)
        send(0, 0)
        send(0, 1)
        blocks(y + 3, 3, 1)

    def gref(m, h, p, q):
        return (m, h, q, p) if h == 0 else (m, h, p, q)

    def rs2(m, h):
        arrived(r1.at[m, h], "r1", m, h)
        for half in range(2):
            to = 1 if half == 0 else -1
            p = at2(h, to)
            for k in range(2):
                at = gref(m, h, p, 2 * half + k)
                grd[at] = (grd[at].astype(F32) + r1[m, h, half, k].astype(F32)).astype(BF)
            src = grd.at[m, h, :, p] if h == 0 else grd.at[m, h, p]
            copy(src, r2.at[m, h, half], ring2(h, to), "r2", m, h)

    def rs3(m, h):
        arrived(r2.at[m, h], "r2", m, h)
        for q in range(4):
            own = grd[gref(m, h, at2(h, 0), q)].astype(F32)
            ysum[m, h, q] = (
                own + r2[m, h, 0, q].astype(F32) + r2[m, h, 1, q].astype(F32)
            ).astype(BF)
        for d in (2, 1, 3):
            copy(ysum.at[m, h, at1(h, d)], r4.at[m, h, d - 1], ring1(h, d), "r4", m, h)

    def deliver(src, u, h, k):
        same = (x == z) & (x == u) & (c == h)
        dst = fin.at[k, z * 2 + c]

        @pl.when(jnp.logical_not(same))
        def _():
            copy(src, dst, {"x": u, "z": x, "c": h}, "hop", k)

        @pl.when(same)
        def _():
            pltpu.make_async_copy(src, dst, sem("hop", k)).start()

    def rs5(m, h):
        arrived(r4.at[m, h], "r4", m, h)
        own = ysum[m, h, at1(h, 0)].astype(F32)
        for d in range(3):
            own = own + r4[m, h, d].astype(F32)
        zed[m, h] = own.astype(BF).reshape(4, 16, 512)
        for u in range(4):
            deliver(zed.at[m, h, u], u, h, 9 + m)

    def landed(k):
        arrived(fin.at[k], "hop", k)


    def mpack(k):
        pack(k)
        xsend(k, 1)

    def mpick(k):
        xwait(k)
        lo, hi = select(k)
        for yy in range(4):
            half = lo if yy < 2 else hi
            mom[k, yy] = half[:, 1024 * (yy % 2) : 1024 * (yy % 2) + 1024]
        yx[k, y] = mom[k, y]
        for d in (1, 3, 2):
            copy(mom.at[k, step4(y, d)], yx.at[k, y], {"y": step4(y, d)}, "y", k)

    def mswap(k):
        if k > 2:
            arrived(yx.at[k, pl.ds(0, 3)], "y", k)
            rows = yx[k].reshape(64, 1024)
        else:
            cols = pl.ds(pl.multiple_of(y * 1024, 1024), 1024)
            rows = wall[k, z, :, :, cols].reshape(64, 1024)
        res = dot(perm64[...], rows).astype(BF)
        for u in range(4):
            for h in range(2):
                swp[k, u, h] = res[16 * u : 16 * u + 16, 512 * h : 512 * h + 512]
                deliver(swp.at[k, u, h], u, h, k)

    def owned(k):
        moved[k] = dot(perm128[...], fin[k].reshape(128, 512)).T.astype(BF)
        pltpu.make_async_copy(moved.at[k], out.at[k], osem).start()

    def mland(k):
        landed(k)
        owned(k)

    def upd(m):
        landed(9 + m)
        owned(9 + m)

    part_in[:, :, 240:, :] = jnp.zeros((3, 3, 16, 256), BF)
    pack_w(1)
    ag1(0)
    pack_w(2)
    mpack(6)
    ag1(1)
    ag2(0, 0, 3)
    mpack(3)
    ag2(0, 1, 3)
    ag2(1, 0, 3)
    ag2(1, 1, 1)
    ag2(1, 1, 2)
    ag2(1, 0, 2)
    ag2(1, 1, 3)
    ag2(1, 0, 1)
    mpack(4)
    fw(1, 0, 0)
    ag2(0, 0, 1)
    mpack(5)
    ag2(0, 1, 1)
    fw(1, 1, 0)
    fw(1, 1, 1)
    ag2(0, 1, 2)
    ag2(0, 0, 2)
    fw(1, 0, 1)
    fw(1, 1, 3)
    fw(1, 1, 2)
    fw(1, 0, 3)
    mpack(7)
    fw(1, 0, 2)
    mpack(8)
    fw(0, 0, 0)
    fw(0, 1, 3)
    fw(0, 1, 0)
    fw(0, 1, 1)
    fw(0, 0, 3)
    fw(0, 0, 2)
    fw(0, 1, 2)
    fw(0, 0, 1)
    ag1(2)
    mpick(5)
    fwd(1)
    fwd(0)
    ag2(2, 0, 2)
    ag2(2, 1, 1)
    ag2(2, 1, 3)
    ag2(2, 1, 2)
    mpick(6)
    ag2(2, 0, 3)
    ag2(2, 0, 1)
    mpick(4)
    fw(2, 0, 0)
    fw(2, 1, 1)
    mswap(1)
    mpick(3)
    fw(2, 1, 3)
    fw(2, 1, 0)
    fw(2, 0, 2)
    fw(2, 0, 1)
    mswap(5)
    fw(2, 1, 2)
    hid()
    fw(2, 0, 3)
    fwd(2)
    mpick(8)
    mswap(0)
    mswap(6)
    bwd(2)
    mswap(8)
    dg(1)
    mpick(7)
    dg(0)
    mswap(4)
    mswap(2)
    rs2(2, 0)
    rs2(2, 1)
    mswap(7)
    bwd(1)
    rs3(2, 1)
    mland(1)
    rs3(2, 0)
    bwd(0)
    rs2(1, 0)
    rs2(1, 1)
    mland(0)
    rs2(0, 0)
    mland(4)
    rs2(0, 1)
    mland(7)
    rs5(2, 1)
    rs3(1, 0)
    rs3(1, 1)
    rs3(0, 1)
    rs3(0, 0)
    mland(6)
    mland(2)
    rs5(2, 0)
    mswap(3)
    rs5(1, 0)
    mland(5)
    mland(8)
    rs5(1, 1)
    rs5(0, 1)
    rs5(0, 0)
    upd(2)
    mland(3)
    upd(1)
    upd(0)
    pltpu.make_async_copy(moved, out, osem).wait()
    left(tok.at[pl.ds(0, 3), pl.ds(0, 240)], "gather")
    left(xs.at[:, pl.ds(0, 3)], "x")
    left(part_in.at[:, :, pl.ds(0, 240)], "part")
    left(part_in, "share")
    left(yx.at[pl.ds(0, 6), pl.ds(0, 3)], "y")
    left(r1, "r1")
    left(r2, "r2")
    left(r4, "r4")
    left(tok.at[:, pl.ds(0, 240)], "sib")

    @pl.when(x == z)
    def _():
        left(fin.at[:, pl.ds(0, 7)], "hop")

    @pl.when(x != z)
    def _():
        left(fin, "hop")

    assert len(received) == NS, len(received)


def on_device(old_weights, old_first, old_second, old_blocks, owner_map, inputs, cotangent):
    any_ = pl.BlockSpec(memory_space=pl.ANY)
    V = pltpu.VMEM
    states = pl.pallas_call(
        kernel,
        out_shape=jax.ShapeDtypeStruct((12, 512, 128), BF),
        in_specs=[any_, any_, any_, any_, any_, any_, any_],
        out_specs=any_,
        scratch_shapes=[
            V((9, 8, 16384), F32),
            V((9, 4, 16, 2048), BF),
            V((9, 4, 16, 2048), BF),
            V((9, 4, 16, 1024), BF),
            V((9, 4, 16, 1024), BF),
            V((9, 4, 2, 16, 512), BF),
            V((12, 8, 16, 512), BF),
            V((3, 4, 4, 16, 4096), BF),
            V((4, 256, 4096), BF),
            V((4, 256, 4096), BF),
            V((3, 4, 256, 256), BF),
            V((3, 3, 256, 256), BF),
            V((3, 4, 256, 256), BF),
            V((3, 2, 4, 4, 64, 512), BF),
            V((3, 2, 2, 2, 64, 512), BF),
            V((3, 2, 2, 4, 64, 512), BF),
            V((3, 2, 4, 64, 512), BF),
            V((3, 2, 3, 64, 512), BF),
            V((3, 2, 4, 16, 512), BF),
            V((16, 64), BF),
            V((16, 64), BF),
            V((256, 256), BF),
            V((64, 64), BF),
            V((128, 128), BF),
            pltpu.SMEM((128,), jnp.int32),
            pltpu.SMEM((4, 128), jnp.int32),
            V((12, 512, 128), BF),
            pltpu.SemaphoreType.DMA((10,)),
            pltpu.SemaphoreType.DMA((NS,)),
            pltpu.SemaphoreType.DMA((15,)),
            pltpu.SemaphoreType.DMA,
        ],
        compiler_params=pltpu.CompilerParams(
            collective_id=0, has_side_effects=True, vmem_limit_bytes=64 * 1024 * 1024
        ),
        name="restore_step",
    )(
        old_blocks, owner_map.T, old_weights, old_first, old_second,
        inputs.reshape(480, 4096), cotangent.reshape(480, 16384),
    )
    w, first, second, grad = (states[3 * i : 3 * i + 3].astype(F32) for i in range(4))
    first = 0.9 * first + 0.1 * grad
    second = 0.95 * second + 0.05 * grad * grad
    w = w - 8e-05 * (first / (jnp.sqrt(second) + 1e-08) + 0.1 * w)
    return tuple(jnp.transpose(o, (1, 0, 2)) for o in (w, first, second))


def solution(mesh):
    grid = Mesh(mesh.devices.reshape(4, 4, 2, 4), ("z", "y", "c", "x"))
    dp = ("z", "y", "c")
    shard = P(None, ("z", "y", "c", "x"), None)
    in_specs = (shard, shard, shard, P(), P(), P(None, dp, "x"), P(None, dp, None))
    out_specs = (P(dp, None, "x"),) * 3
    return jax.shard_map(
        on_device, mesh=grid, in_specs=in_specs, out_specs=out_specs, check_vma=False
    )
```
